128 devices in a mesh: space: 32 (over y, x, core), tm: 4 (over z).
Axes of the slice: x: 4, y: 4, z: 4, core: 2. Of those that a mesh axis runs over, the one named last changes fastest.
Arguments:
- sources: float32 [2, 2, 4, 3, 32, 4, 1024], P(None, None, None, None, 'space', 'tm'), may hold values from -6 to 6
- links: float32 [4, 2, 3, 3, 32, 4, 1024], P(None, None, None, None, 'space', 'tm'), may hold values from -6 to 6
- clover: float32 [2, 2, 6, 6, 32, 4, 1024], P(None, None, None, None, 'space', 'tm'), may hold values from -0.6 to 3.6
- momenta: int32 [33, 3], replicated, may hold values from -3 to 3, as said below
Outputs:
- loops: float32 [2, 32, 33, 4], P(None, 'space', None, 'tm')
The draws below stay inside these ranges and needn't reach their ends.
Inputs may be any that keep to these rules, and one draw needn't show every extreme that they name: `momenta`: no row is the zero vector.
All inputs are finite; a program needn't handle non-finite values.
Results may differ from the reference program's by a relative error of at most 0.0003.
Values sent between devices are 32-bit elements; how exact they have to be, the bound alone decides.
A program may use at most 192 MiB of HBM per device.

```python
import math
import jax
import jax.numpy as jnp
import numpy as np
from jax import lax

NY = 32
NZ = 32
NSRC = 2
NMOM = 33
ITERS = 2
NX = 32
NT = 4
NYZ = 1024


def draw_clover(key, part):
    full_shape = (2, 2, 6, 6, NX, NT, NY * NZ)
    key_off, key_diag = jax.random.split(jax.random.fold_in(key, 11))
    offdiag = 0.15 * jax.random.truncated_normal(key_off, -4.0, 4.0, full_shape, jnp.float32)
    diag_shape = (2, 6, NX, NT, NY * NZ)
    diagonal = jax.random.uniform(key_diag, diag_shape, jnp.float32, 1.0, 2.0)
    identity_six = (lax.broadcasted_iota(jnp.int32, (6, 6), 0) == lax.broadcasted_iota(jnp.int32, (6, 6), 1)).astype(jnp.float32)
    real_part = offdiag[0] + identity_six[None, :, :, None, None, None] * diagonal[:, :, None]
    return jnp.stack([real_part, offdiag[1]], 0).astype(jnp.float32)


def draw_momenta(key, part):
    values = jax.random.randint(jax.random.fold_in(key, 23), (NMOM, 3), -3, 4, dtype=jnp.int32)
    row_index = lax.broadcasted_iota(jnp.int32, (NMOM, 3), 0)
    col_index = lax.broadcasted_iota(jnp.int32, (NMOM, 3), 1)
    zero_row = jnp.all(values == 0, axis=1, keepdims=True)
    values = jnp.where(zero_row & (col_index == 2), 1, values)
    values = jnp.where((row_index == 0) & (col_index == 0), 3, values)
    values = jnp.where((row_index == 1) & (col_index == 0), -3, values)
    return values.astype(jnp.int32)


def steps_of(own_key, extent, pieces, least, largest):
    loudness, own = 1.0, jax.random.fold_in(own_key, 6)
    for dim, parts in pieces:
        steps = jnp.exp(jax.random.uniform(jax.random.fold_in(own, dim), (parts,), jnp.float32, least / len(pieces), largest / len(pieces)))
        loudness = loudness * jnp.repeat(steps, extent[dim] // parts).reshape([-1 if axis == dim else 1 for axis in range(len(extent))])
    return loudness


def bell_draw(key, shape, deviation, limit, cuts=(), kind=jnp.bfloat16):
    level = steps_of(key, shape, cuts, -0.22, 0.18) if cuts else 1.0
    entries = jax.random.normal(key, shape, jnp.float32) * deviation * level
    return jnp.minimum(jnp.maximum(entries, -limit), limit).astype(kind)


def setup_inputs(seed: int = 0) -> dict:
    key_of = jax.random.split(jax.random.key(seed), 5)
    sources = bell_draw(key_of[0], (NSRC, 2, 4, 3, NX, NT, NYZ), 0.7071, 6.0, ((4, 32), (5, 4)), jnp.float32)
    links = bell_draw(key_of[1], (4, 2, 3, 3, NX, NT, NYZ), 0.4082, 6.0, ((4, 32), (5, 4)), jnp.float32)
    clover = draw_clover(jax.random.fold_in(key_of[4], 71), 0)
    momenta = draw_momenta(jax.random.fold_in(key_of[4], 71), 0)
    return {"sources": sources, "links": links, "clover": clover, "momenta": momenta}


KAPPA = 0.1

def gamma_blocks():
    sigma_one = np.array([[0.0, 1.0], [1.0, 0.0]]) + 0j
    sigma_two = np.array([[0.0, -1j], [1j, 0.0]])
    sigma_three = np.array([[1.0, 0.0], [0.0, -1.0]]) + 0j
    identity_two = np.eye(2) + 0j
    upper_blocks = [1j * sigma_one, 1j * sigma_two, 1j * sigma_three, identity_two]
    lower_blocks = [-1j * sigma_one, -1j * sigma_two, -1j * sigma_three, identity_two]
    return (upper_blocks, lower_blocks)

def gamma_tables():
    upper_blocks, lower_blocks = gamma_blocks()
    zero_two = np.zeros((2, 2)) + 0j
    singles = []
    for direction in range(4):
        top_rows = np.concatenate([zero_two, upper_blocks[direction]], axis=1)
        bottom_rows = np.concatenate([lower_blocks[direction], zero_two], axis=1)
        singles.append(np.concatenate([top_rows, bottom_rows], axis=0))
    products = []
    for index_bits in range(16):
        product = np.eye(4) + 0j
        for direction in range(4):
            if index_bits >> direction & 1:
                product = product @ singles[direction]
        products.append(product)
    stacked = np.stack(products)
    return (jnp.asarray(stacked.real, dtype=jnp.float32), jnp.asarray(stacked.imag, dtype=jnp.float32))

def spin_apply(matrix, spinor):
    real_part = spinor[:, 0]
    imag_part = spinor[:, 1]
    rows_re = []
    rows_im = []
    for out_spin in range(matrix.shape[0]):
        acc_re = jnp.zeros_like(real_part[:, 0])
        acc_im = jnp.zeros_like(real_part[:, 0])
        for in_spin in range(matrix.shape[1]):
            coef_re = float(matrix[out_spin, in_spin].real)
            coef_im = float(matrix[out_spin, in_spin].imag)
            if coef_re != 0.0:
                acc_re = acc_re + coef_re * real_part[:, in_spin]
                acc_im = acc_im + coef_re * imag_part[:, in_spin]
            if coef_im != 0.0:
                acc_re = acc_re - coef_im * imag_part[:, in_spin]
                acc_im = acc_im + coef_im * real_part[:, in_spin]
        rows_re.append(acc_re)
        rows_im.append(acc_im)
    return jnp.stack([jnp.stack(rows_re, 1), jnp.stack(rows_im, 1)], 1)

def color_apply(link_mat, spinor, adjoint):
    real_part = spinor[:, 0]
    imag_part = spinor[:, 1]
    rows_re = []
    rows_im = []
    for out_col in range(3):
        acc_re = jnp.zeros_like(real_part[:, :, 0])
        acc_im = jnp.zeros_like(real_part[:, :, 0])
        for in_col in range(3):
            if adjoint:
                entry_re = link_mat[0, in_col, out_col]
                entry_im = -link_mat[1, in_col, out_col]
            else:
                entry_re = link_mat[0, out_col, in_col]
                entry_im = link_mat[1, out_col, in_col]
            src_re = real_part[:, :, in_col]
            src_im = imag_part[:, :, in_col]
            acc_re = acc_re + entry_re * src_re - entry_im * src_im
            acc_im = acc_im + entry_re * src_im + entry_im * src_re
        rows_re.append(acc_re)
        rows_im.append(acc_im)
    return jnp.stack([jnp.stack(rows_re, 2), jnp.stack(rows_im, 2)], 1)

def clover_apply(clover, spinor, adjoint):
    lead_shape = spinor.shape
    blocks = spinor.reshape((lead_shape[0], 2, 2, 6) + lead_shape[4:])
    real_part = blocks[:, 0]
    imag_part = blocks[:, 1]
    rows_re = []
    rows_im = []
    for out_idx in range(6):
        acc_re = jnp.zeros_like(real_part[:, :, 0])
        acc_im = jnp.zeros_like(real_part[:, :, 0])
        for in_idx in range(6):
            if adjoint:
                entry_re = clover[0, :, in_idx, out_idx]
                entry_im = -clover[1, :, in_idx, out_idx]
            else:
                entry_re = clover[0, :, out_idx, in_idx]
                entry_im = clover[1, :, out_idx, in_idx]
            src_re = real_part[:, :, in_idx]
            src_im = imag_part[:, :, in_idx]
            acc_re = acc_re + entry_re * src_re - entry_im * src_im
            acc_im = acc_im + entry_re * src_im + entry_im * src_re
        rows_re.append(acc_re)
        rows_im.append(acc_im)
    joined = jnp.stack([jnp.stack(rows_re, 2), jnp.stack(rows_im, 2)], 1)
    return joined.reshape(lead_shape)

def project(spinor, direction, sign_value):
    upper_blocks, lower_blocks = gamma_blocks()
    matrix = np.concatenate([np.eye(2) + 0j, sign_value * upper_blocks[direction]], axis=1)
    return spin_apply(matrix, spinor)

def reconstruct(half_spinor, direction, sign_value):
    upper_blocks, lower_blocks = gamma_blocks()
    lower_half = spin_apply(sign_value * lower_blocks[direction], half_spinor)
    return jnp.concatenate([half_spinor, lower_half], axis=2)

def gamma_five(spinor):
    return jnp.concatenate([spinor[:, :, :2], -spinor[:, :, 2:]], axis=2)

def roll_plane(spinor, offset, which_axis):
    lead_shape = spinor.shape[:-1]
    grid = spinor.reshape(lead_shape + (NY, NZ))
    grid = jnp.roll(grid, offset, axis=grid.ndim - 2 + which_axis)
    return grid.reshape(lead_shape + (NY * NZ,))

def shift_global(spinor, direction, offset):
    if direction == 0:
        return jnp.roll(spinor, offset, axis=4)
    if direction == 3:
        return jnp.roll(spinor, offset, axis=5)
    return roll_plane(spinor, offset, direction - 1)

def squares(spinor):
    return lax.optimization_barrier(jnp.sum(spinor * spinor, axis=(1, 2, 3, 4, 5, 6)))

def per_source(values):
    return values.reshape((-1, 1, 1, 1, 1, 1, 1))

def reference(sources, links, clover, momenta):
    coord_x = jnp.arange(NX, dtype=jnp.int32)
    coord_t = jnp.arange(NT, dtype=jnp.int32)
    coord_yz = jnp.arange(NY * NZ, dtype=jnp.int32)
    coord_y = coord_yz // NZ
    coord_z = coord_yz % NZ
    parity = (coord_x[:, None, None] + coord_t[None, :, None] + (coord_y + coord_z)[None, None, :]) % 2
    even_mask = (parity == 0).astype(jnp.float32)
    odd_mask = 1.0 - even_mask
    ahead_sign = jnp.where(coord_t == NT - 1, -1.0, 1.0).astype(jnp.float32)[:, None]
    behind_sign = jnp.where(coord_t == 0, -1.0, 1.0).astype(jnp.float32)[:, None]

    def hopping(spinor):
        accumulated = jnp.zeros_like(spinor)
        for direction in range(4):
            link_mat = links[direction]
            ahead_half = shift_global(project(spinor, direction, -1.0), direction, -1)
            if direction == 3:
                ahead_half = ahead_half * ahead_sign
            accumulated = accumulated + reconstruct(color_apply(link_mat, ahead_half, False), direction, -1.0)
            behind_half = shift_global(color_apply(link_mat, project(spinor, direction, 1.0), True), direction, 1)
            if direction == 3:
                behind_half = behind_half * behind_sign
            accumulated = accumulated + reconstruct(behind_half, direction, 1.0)
        return accumulated

    def forward_op(spinor):
        even_in = spinor * even_mask
        inner_field = clover_apply(clover, odd_mask * hopping(even_in), False)
        return clover_apply(clover, even_in, False) - KAPPA * KAPPA * (even_mask * hopping(inner_field))

    def adjoint_op(spinor):
        even_in = spinor * even_mask
        inner_field = clover_apply(clover, odd_mask * hopping(gamma_five(even_in)), True)
        return clover_apply(clover, even_in, True) - KAPPA * KAPPA * (even_mask * gamma_five(hopping(inner_field)))
    even_part = sources * even_mask
    odd_part = sources * odd_mask
    rhs = even_part + KAPPA * (even_mask * hopping(clover_apply(clover, odd_part, False)))
    solution = jnp.zeros_like(rhs)
    residual = adjoint_op(rhs)
    direction_field = residual
    norm_now = squares(residual)
    for iteration in range(ITERS):
        image_field = forward_op(direction_field)
        step_size = norm_now / squares(image_field)
        solution = solution + per_source(step_size) * direction_field
        if iteration + 1 < ITERS:
            residual = residual - per_source(step_size) * adjoint_op(image_field)
            norm_next = squares(residual)
            direction_field = residual + per_source(norm_next / norm_now) * direction_field
            norm_now = norm_next
    psi_field = even_mask * solution + odd_mask * clover_apply(clover, odd_part + KAPPA * hopping(solution), False)
    source_re = sources[:, 0]
    source_im = sources[:, 1]
    psi_re = psi_field[:, 0]
    psi_im = psi_field[:, 1]
    highest = lax.Precision.HIGHEST
    form = 'nacxty,nbcxty->nabxty'
    bilin_re = jnp.einsum(form, source_re, psi_re, precision=highest) + jnp.einsum(form, source_im, psi_im, precision=highest)
    bilin_im = jnp.einsum(form, source_re, psi_im, precision=highest) - jnp.einsum(form, source_im, psi_re, precision=highest)
    gamma_re, gamma_im = gamma_tables()
    gform = 'gab,nabxty->ngxty'
    current_re = jnp.einsum(gform, gamma_re, bilin_re, precision=highest) - jnp.einsum(gform, gamma_im, bilin_im, precision=highest)
    current_im = jnp.einsum(gform, gamma_re, bilin_im, precision=highest) + jnp.einsum(gform, gamma_im, bilin_re, precision=highest)
    frac_x = (momenta[:, 0:1] * coord_x[None, :] % NX).astype(jnp.float32) / NX
    frac_y = (momenta[:, 1:2] * coord_y[None, :] % NY).astype(jnp.float32) / NY
    frac_z = (momenta[:, 2:3] * coord_z[None, :] % NZ).astype(jnp.float32) / NZ
    angles = 2.0 * math.pi * (frac_x[:, :, None] + (frac_y + frac_z)[:, None, :])
    cosines = jnp.cos(angles)
    sines = jnp.sin(angles)
    pform = 'ngxty,pxy->ngpt'
    loop_re = jnp.einsum(pform, current_re, cosines, precision=highest) + jnp.einsum(pform, current_im, sines, precision=highest)
    loop_im = jnp.einsum(pform, current_im, cosines, precision=highest) - jnp.einsum(pform, current_re, sines, precision=highest)
    scale_factor = 1.0 / math.sqrt(NX * NY * NZ)
    joined = jnp.stack([loop_re, loop_im], 0) * scale_factor
    return joined.reshape((2, NSRC * 16, NMOM, NT))
```

```python
import math

import jax
import jax.numpy as jnp
import numpy as np
from jax import lax
from jax.experimental import pallas as pl
from jax.experimental.pallas import tpu as pltpu
from jax.sharding import PartitionSpec as P

MESH = pl.DeviceIdType.MESH
NZ = 32
NY = 32
KAPPA = 0.1
MOM = 48


UPPER = (((1, 1), (0, 1)), ((1, 0), (0, 2)), ((0, 1), (1, 3)), ((0, 0), (1, 0)))
LOWER = (((1, 3), (0, 3)), ((1, 2), (0, 0)), ((0, 3), (1, 1)), ((0, 0), (1, 0)))


def gamma_products():
    sigma = [
        np.array([[0, 1], [1, 0]]) + 0j,
        np.array([[0, -1j], [1j, 0]]),
        np.array([[1, 0], [0, -1]]) + 0j,
    ]
    zero = np.zeros((2, 2)) + 0j
    singles = [np.block([[zero, 1j * s], [-1j * s, zero]]) for s in sigma]
    singles.append(np.block([[zero, np.eye(2)], [np.eye(2), zero]]) + 0j)
    products = []
    for bits in range(16):
        product = np.eye(4) + 0j
        for direction in range(4):
            if bits >> direction & 1:
                product = product @ singles[direction]
        products.append(product)
    return products


def times_i(power, re, im):
    power %= 4
    if power == 0:
        return re, im
    if power == 1:
        return -im, re
    if power == 2:
        return -re, -im
    return im, -re


def add_times_i(power, acc, term):
    (ar, ai), (re, im) = acc, term
    power %= 4
    if power == 0:
        return ar + re, ai + im
    if power == 1:
        return ar - im, ai + re
    if power == 2:
        return ar - re, ai - im
    return ar + im, ai - re


def color_apply(link, half, adjoint):
    hr, hi = half
    outr = outi = None
    for b in range(3):
        if adjoint:
            ur, ui = link[0, b], link[1, b]
        else:
            ur, ui = link[0, :, b], link[1, :, b]
        ur, ui = ur[None], ui[None]
        xr, xi = hr[:, b][:, None], hi[:, b][:, None]
        if adjoint:
            tr, ti = ur * xr + ui * xi, ur * xi - ui * xr
        else:
            tr, ti = ur * xr - ui * xi, ur * xi + ui * xr
        outr, outi = (tr, ti) if outr is None else (outr + tr, outi + ti)
    return outr, outi


def clover_apply(mat, fr, fi):
    xr, xi = fr.reshape(2, 6, 8, 128), fi.reshape(2, 6, 8, 128)
    outr = outi = None
    for i in range(6):
        cr, ci = mat[0, :, :, i], mat[1, :, :, i]
        vr, vi = xr[:, i][:, None], xi[:, i][:, None]
        tr, ti = cr * vr - ci * vi, cr * vi + ci * vr
        outr, outi = (tr, ti) if outr is None else (outr + tr, outi + ti)
    return outr.reshape(4, 3, 8, 128), outi.reshape(4, 3, 8, 128)


def kernel(
    n_space, n_tm,
    src_hbm, link_hbm, clov_hbm, mom_ref, out_ref,
    src, link, clov, wlink, wclov, sfield, field, inner, bil, cur, phase_hi, phase_lo, momrow,
    send, recv, norm_a, norm_ar, norm_b, norm_br, norm_t, loop_s, loop_r,
    in_sem, send_sem, recv_sem, norm_ssem, norm_rsem, loop_ssem, loop_rsem,
):
    x = lax.axis_index("space")
    t = lax.axis_index("tm")
    x_up, x_dn = lax.rem(x + 1, n_space), lax.rem(x + n_space - 1, n_space)
    t_up, t_dn = lax.rem(t + 1, n_tm), lax.rem(t + n_tm - 1, n_tm)

    loads = [
        pltpu.make_async_copy(a, b, in_sem.at[k])
        for k, (a, b) in enumerate(((src_hbm, src), (clov_hbm, clov), (link_hbm, link)))
    ]
    for load in loads:
        load.start()

    barrier = pltpu.get_barrier_semaphore()

    def greet_space(d, carry):
        pl.semaphore_signal(barrier, inc=1, device_id=(lax.rem(x + d, n_space), t), device_id_type=MESH)
        return carry

    lax.fori_loop(1, n_space, greet_space, 0)
    for d in range(1, n_tm):
        pl.semaphore_signal(barrier, inc=1, device_id=(x, lax.rem(t + d, n_tm)), device_id_type=MESH)

    lane = lax.broadcasted_iota(jnp.int32, (8, 128), 1)
    row = lax.broadcasted_iota(jnp.int32, (8, 128), 0)
    zc = lane & 31
    yc = row * 4 + (lane >> 5)
    ev = ((yc + zc + x + t) & 1) == 0
    low_rows = row < 4

    def move(v, axis, by):
        if axis == 2:
            last = v.ndim - 1
            if by == 1:
                return jnp.where(zc == 31, pltpu.roll(v, 31, last), pltpu.roll(v, 127, last))
            return jnp.where(zc == 0, pltpu.roll(v, 97, last), pltpu.roll(v, 1, last))
        if by == 1:
            a = pltpu.roll(v, 96, v.ndim - 1)
            return jnp.where(lane >= 96, pltpu.roll(a, 7, v.ndim - 2), a)
        a = pltpu.roll(v, 32, v.ndim - 1)
        return jnp.where(lane < 32, pltpu.roll(a, 1, v.ndim - 2), a)

    mom = mom_ref[...].astype(jnp.float32)
    n_mom = mom.shape[1]
    eye = lax.broadcasted_iota(jnp.int32, (MOM, n_mom), 0) == lax.broadcasted_iota(jnp.int32, (MOM, n_mom), 1)
    columns = [
        jnp.sum(jnp.where(eye, jnp.broadcast_to(mom[k : k + 1], (MOM, n_mom)), 0.0), axis=1, keepdims=True).astype(jnp.int32)
        for k in range(3)
    ]

    def cos_sin(k):
        a = (k - 16).astype(jnp.float32) * (math.pi / 32)
        q = a * a
        s = 1.0 / math.factorial(11)
        for m in (9, 7, 5, 3, 1):
            s = 1.0 / math.factorial(m) - q * s
        s = s * a
        c = 1.0 / math.factorial(12)
        for m in (10, 8, 6, 4, 2, 0):
            c = 1.0 / math.factorial(m) - q * c
        return 2.0 * s * s - 1.0, -2.0 * s * c

    zero_rows = jnp.zeros((64 - MOM, 2048), jnp.bfloat16)
    for ref in (phase_hi, phase_lo):
        ref[MOM:64, :] = zero_rows
        ref[64 + MOM : 128, :] = zero_rows

    lane1 = lax.broadcasted_iota(jnp.int32, (1, 128), 1)

    def phases(s, carry):
        yrow = s * 4 + (lane1 >> 5)
        zrow = lane1 & 31
        k = (columns[0] * x + columns[1] * yrow + columns[2] * zrow) & 31
        c, sn = cos_sin(k)
        for value, places in ((c, ((0, 0, 1), (64, 128, 1))), (sn, ((0, 128, 1), (64, 0, -1)))):
            for r0, c0, sign in places:
                v = value if sign == 1 else -value
                hi = v.astype(jnp.bfloat16)
                at = pl.ds(pl.multiple_of(s * 256 + c0, 128), 128)
                phase_hi[r0 : r0 + MOM, at] = hi
                phase_lo[r0 : r0 + MOM, at] = (v - hi.astype(jnp.float32)).astype(jnp.bfloat16)
        return carry

    lax.fori_loop(0, 8, phases, 0)

    momrow[...] = jnp.zeros_like(momrow)
    momrow[0:1, 0:n_mom] = mom[2:3]
    momrow[0:1, 64 : 64 + n_mom] = mom[2:3]
    loop_s[...] = jnp.zeros_like(loop_s)

    loads[0].wait()
    for re_im in range(2):
        a = src[0, re_im]
        b = move(src[1, re_im], 2, -1)
        sfield[0, re_im] = jnp.where(ev, a, b)
        sfield[1, re_im] = jnp.where(ev, b, a)

    loads[1].wait()

    def pack_clover(k, carry):
        re_im, chi, r = k // 12, (k // 6) % 2, k % 6
        sign = (1 - 2 * re_im).astype(jnp.float32)
        a = clov[re_im, chi, r]
        b = move(a, 2, -1)
        for par, v in ((0, jnp.where(ev, a, b)), (1, jnp.where(ev, b, a))):
            wclov[1, par, re_im, chi, r] = v
            wclov[0, par, re_im, chi, :, r] = v * sign
        return carry

    lax.fori_loop(0, 24, pack_clover, 0)

    loads[2].wait()
    t_sign = jnp.where(t == n_tm - 1, -1.0, 1.0).astype(jnp.float32)

    def pack_links(k, carry):
        mu, re_im = k // 2, k % 2
        a = link[mu, re_im] * jnp.where(mu == 3, t_sign, 1.0)
        b = move(a, 2, -1)
        wlink[0, mu, re_im] = jnp.where(ev, a, b)
        wlink[1, mu, re_im] = jnp.where(ev, b, a)
        return carry

    lax.fori_loop(0, 8, pack_links, 0)

    pl.semaphore_wait(barrier, n_space - 1 + n_tm - 1)

    ROUTES = ((3, -1, (x, t_dn)), (0, -1, (x_dn, t)), (3, 1, (x, t_up)), (0, 1, (x_up, t)))

    def halo(j, k):
        return pltpu.make_async_remote_copy(
            src_ref=send.at[j, k], dst_ref=recv.at[j, k], send_sem=send_sem, recv_sem=recv_sem.at[j, k],
            device_id=ROUTES[k][2], device_id_type=MESH,
        )

    def project(fr, fi, mu, sign):
        rows_r, rows_i = [], []
        for spin in range(2):
            col, power = UPPER[mu][spin]
            if sign < 0:
                power += 2
            r, i = add_times_i(power, (fr[spin], fi[spin]), (fr[2 + col], fi[2 + col]))
            rows_r.append(r)
            rows_i.append(i)
        return jnp.stack(rows_r), jnp.stack(rows_i)

    def add_up(acc, half, mu, sign):
        hr, hi = half
        for spin in range(2):
            acc[spin] = (hr[spin], hi[spin]) if acc[spin] is None else (acc[spin][0] + hr[spin], acc[spin][1] + hi[spin])
            col, power = LOWER[mu][spin]
            if sign < 0:
                power += 2
            term = (hr[col], hi[col])
            acc[2 + spin] = times_i(power, *term) if acc[2 + spin] is None else add_times_i(power, acc[2 + spin], term)

    def hop(j, par, fr, fi, early, late):
        to = 1 - par
        for k, (mu, sign, _) in enumerate(ROUTES):
            half = project(fr, fi, mu, sign)
            if sign > 0:
                half = color_apply(wlink.at[par, mu], half, True)
            send[j, k, 0] = half[0]
            send[j, k, 1] = half[1]
            halo(j, k).start()
        early()
        acc = [None] * 4
        for mu in (1, 2):
            hr, hi = project(fr, fi, mu, -1)
            ahead = (move(hr, mu, 1), move(hi, mu, 1))
            add_up(acc, color_apply(wlink.at[to, mu], ahead, False), mu, -1)
            hr, hi = color_apply(wlink.at[par, mu], project(fr, fi, mu, 1), True)
            add_up(acc, (move(hr, mu, -1), move(hi, mu, -1)), mu, 1)
        late()
        for k, (mu, sign, _) in enumerate(ROUTES):
            halo(j, k).wait_recv()
            half = (recv[j, k, 0], recv[j, k, 1])
            if sign < 0:
                half = color_apply(wlink.at[to, mu], half, False)
            add_up(acc, half, mu, sign)
        return jnp.stack([a[0] for a in acc]), jnp.stack([a[1] for a in acc])

    def norm_local(p, fr, fi):
        sq = jnp.sum(fr * fr + fi * fi, axis=(0, 1))
        e, o = jnp.where(ev, sq, 0.0), jnp.where(ev, 0.0, sq)
        norm_a[p] = jnp.where(low_rows, e + pltpu.roll(e, 4, 0), o + pltpu.roll(o, 4, 0))

    def norm_send_a(p):
        for d in range(1, n_tm):
            pltpu.make_async_remote_copy(
                src_ref=norm_a.at[p], dst_ref=norm_ar.at[p, n_tm - 1 - d], send_sem=norm_ssem.at[p, 0],
                recv_sem=norm_rsem.at[p, 0], device_id=(x, lax.rem(t + d, n_tm)), device_id_type=MESH,
            ).start()

    def norm_recv_a(p):
        whole = norm_ar.at[p]
        pltpu.make_async_copy(whole, whole, norm_rsem.at[p, 0]).wait()
        norm_b[p] = norm_a[p] + jnp.sum(norm_ar[p], axis=0)

    def norm_send_b(p):
        def step(d, carry):
            pltpu.make_async_remote_copy(
                src_ref=norm_b.at[p], dst_ref=norm_br.at[p, n_space - 1 - d], send_sem=norm_ssem.at[p, 1],
                recv_sem=norm_rsem.at[p, 1], device_id=(lax.rem(x + d, n_space), t), device_id_type=MESH,
            ).start()
            return carry

        lax.fori_loop(1, n_space, step, 0)

    def norm_recv_b(p):
        whole = norm_br.at[p]
        pltpu.make_async_copy(whole, whole, norm_rsem.at[p, 1]).wait()
        norm_t[p] = norm_b[p] + jnp.sum(norm_br[p], axis=0)

    def total(p):
        v = norm_t[p]
        both = []
        for part in (jnp.where(low_rows, v, 0.0), jnp.where(low_rows, 0.0, v)):
            both.append(jnp.sum(jnp.sum(part, axis=0, keepdims=True), axis=1, keepdims=True))
        return both

    def spread(pair):
        return jnp.where(ev, jnp.broadcast_to(pair[0], (8, 128)), jnp.broadcast_to(pair[1], (8, 128)))

    products = gamma_products()

    def project_loops(q, at_field, at_inner):
        for a in range(4):
            par_r, par_i = [], []
            for par, ref, at in ((0, field, at_field), (1, inner, at_inner)):
                br = bi = None
                for c in range(3):
                    sr, si = sfield[par, 0, a, c], sfield[par, 1, a, c]
                    pr, pi = ref[at, 0, :, c], ref[at, 1, :, c]
                    tr, ti = sr * pr + si * pi, sr * pi - si * pr
                    br, bi = (tr, ti) if br is None else (br + tr, bi + ti)
                par_r.append(br)
                par_i.append(bi)
            for re_im, (e, o) in enumerate((par_r, par_i)):
                bil[0, re_im, a] = jnp.where(ev, e, o)
                bil[1, re_im, a] = jnp.where(ev, o, e)

        def gammas(n, carry):
            for first in range(4):
                group = [g for g in range(16) if abs(products[g][0, first]) > 0.5]
                perm = [int(np.argmax(np.abs(products[group[0]][a]))) for a in range(4)]
                terms = [(bil[n, 0, a, perm[a]], bil[n, 1, a, perm[a]]) for a in range(4)]
                for g in group:
                    acc = None
                    for a in range(4):
                        power = int(round(np.angle(products[g][a, perm[a]]) / (math.pi / 2))) % 4
                        acc = times_i(power, *terms[a]) if acc is None else add_times_i(power, acc, terms[a])
                    for re_im in range(2):
                        start = pl.multiple_of((re_im * 32 + n * 16 + g) * 8, 8)
                        cur[pl.ds(start, 8), :] = acc[re_im]
            return carry

        lax.fori_loop(0, 2, gammas, 0)
        out = jnp.zeros((32, 128), jnp.float32)
        contract = (((1,), (1,)), ((), ()))
        for s in range(8):
            both = jnp.concatenate([cur[pl.ds(s, 32, stride=8), :], cur[pl.ds(256 + s, 32, stride=8), :]], axis=1)
            hi = both.astype(jnp.bfloat16)
            lo = (both - hi.astype(jnp.float32)).astype(jnp.bfloat16)
            wide = slice(s * 256, s * 256 + 256)
            ph, plo = phase_hi[:, wide], phase_lo[:, wide]
            main = lax.dot_general(jnp.concatenate([hi, lo], axis=0), ph, contract, preferred_element_type=jnp.float32)
            out = out + main[:32] + main[32:]
            out = out + lax.dot_general(hi, plo, contract, preferred_element_type=jnp.float32)
        loop_s[pl.ds(q, 32, stride=8), :] = out

    def loops_send():
        def step(d, carry):
            target = lax.rem(x + d, n_space)
            pltpu.make_async_remote_copy(
                src_ref=loop_s.at[pl.ds(pl.multiple_of(target * 8, 8), 8)], dst_ref=loop_r.at[n_space - 1 - d],
                send_sem=loop_ssem, recv_sem=loop_rsem, device_id=(target, t), device_id_type=MESH,
            ).start()
            return carry

        lax.fori_loop(1, n_space, step, 0)

    def nothing():
        pass

    zero = jnp.zeros((4, 3, 8, 128), jnp.float32)
    field[5, 0] = zero
    field[5, 1] = zero
    cr, ci = clover_apply(wclov.at[1, 1], sfield[1, 0], sfield[1, 1])
    inner[4, 0] = cr
    inner[4, 1] = ci
    hr, hi = hop(0, 1, cr, ci, nothing, nothing)
    field[0, 0] = sfield[0, 0] + KAPPA * hr
    field[0, 1] = sfield[0, 1] + KAPPA * hi

    def pair(p, carry):
        forward = p % 2
        g5 = (2 * forward - 1).astype(jnp.float32)
        later = p > 0

        def flip(v):
            return jnp.concatenate([v[:2], v[2:] * g5], axis=0)

        def early_a():
            @pl.when(later)
            def _():
                norm_send_a(p - 1)

        def late_b():
            @pl.when(later)
            def _():
                q = p - 1
                project_loops(q, jnp.where(q == 0, 5, 2 * q - 1), jnp.where(q == 0, 4, 2 * q - 1))

            @pl.when(p == 3)
            def _():
                loops_send()

        def early_b():
            @pl.when(later)
            def _():
                norm_recv_a(p - 1)
                norm_send_b(p - 1)

        fr, fi = field[p, 0], field[p, 1]
        hr, hi = hop(2 * p + 1, 0, flip(fr), flip(fi), early_a, nothing)
        vr, vi = clover_apply(wclov.at[forward, 1], hr, hi)
        vr, vi = KAPPA * vr, KAPPA * vi
        inner[p, 0] = vr
        inner[p, 1] = vi
        hr, hi = hop(2 * p + 2, 1, vr, vi, early_b, late_b)
        cr, ci = clover_apply(wclov.at[forward, 0], field[p, 0], field[p, 1])
        outr, outi = cr - KAPPA * flip(hr), ci - KAPPA * flip(hi)
        field[p + 1, 0] = outr
        field[p + 1, 1] = outi

        @pl.when(later)
        def _():
            norm_recv_b(p - 1)

        @pl.when(p == 2)
        def _():
            rr, image = total(0), total(1)
            alpha = spread([rr[n] / image[n] for n in range(2)])
            for re_im in range(2):
                field[3, re_im] = field[1, re_im] - alpha * field[3, re_im]

        @pl.when(p == 3)
        def _():
            new, rr = total(2), total(0)
            beta = spread([new[n] / rr[n] for n in range(2)])
            for re_im in range(2):
                field[4, re_im] = field[4, re_im] + beta * field[2, re_im]

        norm_local(p, field[p + 1, 0], field[p + 1, 1])
        return carry

    lax.fori_loop(0, 4, pair, 0)

    norm_send_a(3)
    norm_recv_a(3)
    norm_send_b(3)
    pltpu.make_async_copy(loop_r, loop_r, loop_rsem).wait()
    own = loop_s[pl.ds(pl.multiple_of(x * 8, 8), 8), :]
    piece = own + jnp.sum(loop_r[...], axis=0)
    second = x >= n_space // 2
    angle = momrow[0:1, :].astype(jnp.int32) * second.astype(jnp.int32)
    cos, sin = cos_sin(angle & 31)
    sin = jnp.where(lane1 < 64, -sin, sin)
    norm_recv_b(3)

    rr0, im0, rr1, im1 = [jnp.where(second, pair_[1], pair_[0]) for pair_ in (total(0), total(1), total(2), total(3))]
    alpha0, alpha1, beta = rr0 / im0, rr1 / im1, rr1 / rr0
    line = piece[0:1] + (alpha0 + alpha1 * beta) * piece[1:2] + alpha1 * piece[2:3]
    line = (line * cos + pltpu.roll(line, 64, 1) * sin) * (1.0 / math.sqrt(n_space * NY * NZ))
    out_ref[0] = line[:, 0:n_mom]
    out_ref[1] = line[:, 64 : 64 + n_mom]

    pltpu.make_async_copy(send, send, send_sem).wait()
    for p in range(4):
        for stage, ref in enumerate((norm_ar, norm_br)):
            pltpu.make_async_copy(ref.at[p], ref.at[p], norm_ssem.at[p, stage]).wait()
    pltpu.make_async_copy(loop_r, loop_r, loop_ssem).wait()


def solution(mesh):
    n_space, n_tm = mesh.shape["space"], mesh.shape["tm"]

    def local(sources, links, clover, momenta):
        f32 = jnp.float32
        n_mom = momenta.shape[0]
        tile = (8, 128)
        scratch = [
            pltpu.VMEM((2, 2, 4, 3) + tile, f32),
            pltpu.VMEM((4, 2, 3, 3) + tile, f32),
            pltpu.VMEM((2, 2, 6, 6) + tile, f32),
            pltpu.VMEM((2, 4, 2, 3, 3) + tile, f32),
            pltpu.VMEM((2, 2, 2, 2, 6, 6) + tile, f32),
            pltpu.VMEM((2, 2, 4, 3) + tile, f32),
            pltpu.VMEM((6, 2, 4, 3) + tile, f32),
            pltpu.VMEM((5, 2, 4, 3) + tile, f32),
            pltpu.VMEM((2, 2, 4, 4) + tile, f32),
            pltpu.VMEM((512, 128), f32),
            pltpu.VMEM((128, 2048), jnp.bfloat16),
            pltpu.VMEM((128, 2048), jnp.bfloat16),
            pltpu.VMEM(tile, f32),
            pltpu.VMEM((9, 4, 2, 2, 3) + tile, f32),
            pltpu.VMEM((9, 4, 2, 2, 3) + tile, f32),
            pltpu.VMEM((4,) + tile, f32),
            pltpu.VMEM((4, n_tm - 1) + tile, f32),
            pltpu.VMEM((4,) + tile, f32),
            pltpu.VMEM((4, n_space - 1) + tile, f32),
            pltpu.VMEM((4,) + tile, f32),
            pltpu.VMEM((256, 128), f32),
            pltpu.VMEM((n_space - 1,) + tile, f32),
            pltpu.SemaphoreType.DMA((3,)),
            pltpu.SemaphoreType.DMA,
            pltpu.SemaphoreType.DMA((9, 4)),
            pltpu.SemaphoreType.DMA((4, 2)),
            pltpu.SemaphoreType.DMA((4, 2)),
            pltpu.SemaphoreType.DMA,
            pltpu.SemaphoreType.DMA,
        ]
        out = pl.pallas_call(
            lambda *refs: kernel(n_space, n_tm, *refs),
            out_shape=jax.ShapeDtypeStruct((2, 1, n_mom), f32),
            in_specs=[pl.BlockSpec(memory_space=pl.ANY)] * 3 + [pl.BlockSpec(memory_space=pltpu.VMEM)],
            out_specs=pl.BlockSpec(memory_space=pltpu.VMEM),
            scratch_shapes=scratch,
            compiler_params=pltpu.CompilerParams(
                collective_id=0, has_side_effects=True, vmem_limit_bytes=32 * 1024 * 1024
            ),
            name="loops",
        )(
            sources.reshape((2, 2, 4, 3) + tile),
            links.reshape((4, 2, 3, 3) + tile),
            clover.reshape((2, 2, 6, 6) + tile),
            momenta.T,
        )
        return out.reshape(2, 1, n_mom, 1)

    placed = P(None, None, None, None, "space", "tm", None)
    return jax.shard_map(
        local, mesh=mesh, in_specs=(placed, placed, placed, P()), out_specs=P(None, "space", None, "tm"), check_vma=False
    )
```

```python
import math

import jax
import jax.numpy as jnp
import numpy as np
from jax import lax
from jax.experimental import pallas as pl
from jax.experimental.pallas import tpu as pltpu
from jax.sharding import PartitionSpec as P

MESH = pl.DeviceIdType.MESH
NZ = 32
NY = 32
KAPPA = 0.1
MOM = 48
UNROLL = True


UPPER = (((1, 1), (0, 1)), ((1, 0), (0, 2)), ((0, 1), (1, 3)), ((0, 0), (1, 0)))
LOWER = (((1, 3), (0, 3)), ((1, 2), (0, 0)), ((0, 3), (1, 1)), ((0, 0), (1, 0)))


def gamma_products():
    sigma = [
        np.array([[0, 1], [1, 0]]) + 0j,
        np.array([[0, -1j], [1j, 0]]),
        np.array([[1, 0], [0, -1]]) + 0j,
    ]
    zero = np.zeros((2, 2)) + 0j
    singles = [np.block([[zero, 1j * s], [-1j * s, zero]]) for s in sigma]
    singles.append(np.block([[zero, np.eye(2)], [np.eye(2), zero]]) + 0j)
    products = []
    for bits in range(16):
        product = np.eye(4) + 0j
        for direction in range(4):
            if bits >> direction & 1:
                product = product @ singles[direction]
        products.append(product)
    return products


def times_i(power, re, im):
    power %= 4
    if power == 0:
        return re, im
    if power == 1:
        return -im, re
    if power == 2:
        return -re, -im
    return im, -re


def add_times_i(power, acc, term):
    (ar, ai), (re, im) = acc, term
    power %= 4
    if power == 0:
        return ar + re, ai + im
    if power == 1:
        return ar - im, ai + re
    if power == 2:
        return ar - re, ai - im
    return ar + im, ai - re


def color_apply(link, half, adjoint):
    hr, hi = half
    outr = outi = None
    for b in range(3):
        if adjoint:
            ur, ui = link[0, b], link[1, b]
        else:
            ur, ui = link[0, :, b], link[1, :, b]
        ur, ui = ur[None], ui[None]
        xr, xi = hr[:, b][:, None], hi[:, b][:, None]
        if adjoint:
            tr, ti = ur * xr + ui * xi, ur * xi - ui * xr
        else:
            tr, ti = ur * xr - ui * xi, ur * xi + ui * xr
        outr, outi = (tr, ti) if outr is None else (outr + tr, outi + ti)
    return outr, outi


def clover_apply(mat, fr, fi):
    xr, xi = fr.reshape(2, 6, 8, 128), fi.reshape(2, 6, 8, 128)
    outr = outi = None
    for i in range(6):
        cr, ci = mat[0, :, :, i], mat[1, :, :, i]
        vr, vi = xr[:, i][:, None], xi[:, i][:, None]
        tr, ti = cr * vr - ci * vi, cr * vi + ci * vr
        outr, outi = (tr, ti) if outr is None else (outr + tr, outi + ti)
    return outr.reshape(4, 3, 8, 128), outi.reshape(4, 3, 8, 128)


def fan(ys, xs, cores, zs):
    offsets = [(y, x, c, z) for y in ys for x in xs for c in cores for z in zs if (y, x, c, z) != (0, 0, 0, 0)]
    return sorted(offsets, key=lambda o: -(min(o[0], 4 - o[0]) + min(o[1], 4 - o[1]) + min(o[3], 4 - o[3])))


ALONG_ROW = fan([0], range(4), range(2), [0])
ALONG_Y = fan(range(4), [0], [0], [0])
ALONG_Z = fan([0], [0], [0], range(4))
ALONG_SPACE = fan(range(4), range(4), range(2), [0])
ROUNDS = (ALONG_ROW, ALONG_Y, ALONG_Z)


def when(condition):
    if isinstance(condition, bool):
        return (lambda f: f()) if condition else (lambda f: None)
    return pl.when(condition)


def pick(condition, a, b):
    if isinstance(condition, bool):
        return a if condition else b
    return jnp.where(condition, a, b)


def kernel(
    n_space, n_tm,
    src_hbm, clov_hbm, link_hbm, mom_hbm, out_ref,
    src, clov, link, mom_ref, wlink, wclov, sfield, field, inner, base, bil, cur, phase_hi, phase_lo, momrow,
    send, recv, row_s, row_r0, row_r1, row_r2, last_r1, last_r2, alpha_ref, loop_s, loop_r,
    in_sem, send_sem, recv_sem, row_ssem, row_rsem, loop_ssem, loop_rsem,
):
    x = lax.axis_index("space")
    t = lax.axis_index("tm")
    x_up, x_dn = lax.rem(x + 1, n_space), lax.rem(x + n_space - 1, n_space)
    t_up, t_dn = lax.rem(t + 1, n_tm), lax.rem(t + n_tm - 1, n_tm)

    loads = [
        pltpu.make_async_copy(a, b, in_sem.at[k])
        for k, (a, b) in enumerate(((src_hbm, src), (clov_hbm, clov), (link_hbm, link), (mom_hbm, mom_ref)))
    ]
    for load in loads:
        load.start()

    def space_at(dy, dx, dc):
        return ((x // 8 + dy) & 3) * 8 + (((x // 2) + dx) & 3) * 2 + ((x + dc) & 1)

    def place(offset):
        dy, dx, dc, dz = offset
        return (space_at(dy, dx, dc), (t + dz) & 3)

    barrier = pltpu.get_barrier_semaphore()
    greeted = ALONG_SPACE + ALONG_Z
    for offset in greeted:
        pl.semaphore_signal(barrier, inc=1, device_id=place(offset), device_id_type=MESH)

    lane = lax.broadcasted_iota(jnp.int32, (8, 128), 1)
    row = lax.broadcasted_iota(jnp.int32, (8, 128), 0)
    lane1 = lax.broadcasted_iota(jnp.int32, (1, 128), 1)
    zc = lane & 31
    yc = row * 4 + (lane >> 5)
    ev = ((yc + zc + x + t) & 1) == 0

    def move(v, axis, by):
        last = v.ndim - 1
        if axis == 2:
            if by == 1:
                return jnp.where(zc == 31, pltpu.roll(v, 31, last), pltpu.roll(v, 127, last))
            return jnp.where(zc == 0, pltpu.roll(v, 97, last), pltpu.roll(v, 1, last))
        if by == 1:
            a = pltpu.roll(v, 96, last)
            return jnp.where(lane >= 96, pltpu.roll(a, 7, last - 1), a)
        a = pltpu.roll(v, 32, last)
        return jnp.where(lane < 32, pltpu.roll(a, 1, last - 1), a)

    def cos_sin(k):
        a = (k - 16).astype(jnp.float32) * (math.pi / 32)
        q = a * a
        s = 1.0 / math.factorial(11)
        for m in (9, 7, 5, 3, 1):
            s = 1.0 / math.factorial(m) - q * s
        s = s * a
        c = 1.0 / math.factorial(12)
        for m in (10, 8, 6, 4, 2, 0):
            c = 1.0 / math.factorial(m) - q * c
        return 2.0 * s * s - 1.0, -2.0 * s * c

    def pack_clover(entries):
        def step(k, carry):
            re_im, chi, r = k // 12, (k // 6) % 2, k % 6
            sign = (1 - 2 * re_im).astype(jnp.float32)
            a = clov[re_im, chi, r]
            b = move(a, 2, -1)
            for forward, par in entries:
                v = jnp.where(ev, a, b) if par == 0 else jnp.where(ev, b, a)
                if forward:
                    wclov[1, par, re_im, chi, r] = v
                else:
                    wclov[0, par, re_im, chi, :, r] = v * sign
            return carry

        lax.fori_loop(0, 24, step, 0)

    t_sign = jnp.where(t == n_tm - 1, -1.0, 1.0).astype(jnp.float32)

    def pack_links(directions):
        for mu in directions:
            for re_im in range(2):
                a = link[mu, re_im]
                if mu == 3:
                    a = a * t_sign
                b = move(a, 2, -1)
                wlink[0, mu, re_im] = jnp.where(ev, a, b)
                wlink[1, mu, re_im] = jnp.where(ev, b, a)

    n_mom = mom_ref.shape[1]

    def make_phases():
        loads[3].wait()
        mom = mom_ref[...].astype(jnp.float32)
        eye = lax.broadcasted_iota(jnp.int32, (MOM, n_mom), 0) == lax.broadcasted_iota(jnp.int32, (MOM, n_mom), 1)
        columns = [
            jnp.sum(jnp.where(eye, jnp.broadcast_to(mom[k : k + 1], (MOM, n_mom)), 0.0), axis=1, keepdims=True).astype(jnp.int32)
            for k in range(3)
        ]
        zero_rows = jnp.zeros((64 - MOM, 2048), jnp.bfloat16)
        for ref in (phase_hi, phase_lo):
            ref[MOM:64, :] = zero_rows
            ref[64 + MOM : 128, :] = zero_rows

        def phases(s, carry):
            yrow = s * 4 + (lane1 >> 5)
            zrow = lane1 & 31
            c, sn = cos_sin((columns[0] * x + columns[1] * yrow + columns[2] * zrow) & 31)
            for value, places in ((c, ((0, 0, 1), (64, 128, 1))), (sn, ((0, 128, 1), (64, 0, -1)))):
                hi = value.astype(jnp.bfloat16)
                lo = (value - hi.astype(jnp.float32)).astype(jnp.bfloat16)
                for r0, c0, sign in places:
                    at = pl.ds(pl.multiple_of(s * 256 + c0, 128), 128)
                    phase_hi[r0 : r0 + MOM, at] = hi * sign
                    phase_lo[r0 : r0 + MOM, at] = lo * sign
            return carry

        lax.fori_loop(0, 8, phases, 0)
        momrow[...] = jnp.zeros_like(momrow)
        momrow[0:1, 0:n_mom] = mom[2:3]
        momrow[0:1, 64 : 64 + n_mom] = mom[2:3]
        loop_s[...] = jnp.zeros_like(loop_s)
        zero = jnp.zeros((4, 3, 8, 128), jnp.float32)
        field[5, 0] = zero
        field[5, 1] = zero

    ROUTES = ((0, -1, (x_dn, t)), (0, 1, (x_up, t)), (3, -1, (x, t_dn)), (3, 1, (x, t_up)))

    def halo(j, k):
        return pltpu.make_async_remote_copy(
            src_ref=send.at[j, k], dst_ref=recv.at[j, k], send_sem=send_sem, recv_sem=recv_sem.at[j, k],
            device_id=ROUTES[k][2], device_id_type=MESH,
        )

    def project(fr, fi, mu, sign):
        rows_r, rows_i = [], []
        for spin in range(2):
            col, power = UPPER[mu][spin]
            if sign < 0:
                power += 2
            r, i = add_times_i(power, (fr[spin], fi[spin]), (fr[2 + col], fi[2 + col]))
            rows_r.append(r)
            rows_i.append(i)
        return jnp.stack(rows_r), jnp.stack(rows_i)

    def add_up(acc, half, mu, sign):
        hr, hi = half
        for spin in range(2):
            acc[spin] = (hr[spin], hi[spin]) if acc[spin] is None else (acc[spin][0] + hr[spin], acc[spin][1] + hi[spin])
            col, power = LOWER[mu][spin]
            if sign < 0:
                power += 2
            term = (hr[col], hi[col])
            acc[2 + spin] = times_i(power, *term) if acc[2 + spin] is None else add_times_i(power, acc[2 + spin], term)

    def hop(j, par, fr, fi, early, late):
        to = 1 - par
        for k, (mu, sign, _) in enumerate(ROUTES):
            half = project(fr, fi, mu, sign)
            if sign > 0:
                half = color_apply(wlink.at[par, mu], half, True)
            send[j, k, 0] = half[0]
            send[j, k, 1] = half[1]
            halo(j, k).start()
        early()
        acc = [None] * 4
        for mu in (1, 2):
            hr, hi = project(fr, fi, mu, -1)
            ahead = (move(hr, mu, 1), move(hi, mu, 1))
            add_up(acc, color_apply(wlink.at[to, mu], ahead, False), mu, -1)
            hr, hi = color_apply(wlink.at[par, mu], project(fr, fi, mu, 1), True)
            add_up(acc, (move(hr, mu, -1), move(hi, mu, -1)), mu, 1)
        late()
        for k in (2, 3, 0, 1):
            mu, sign, _ = ROUTES[k]
            halo(j, k).wait_recv()
            half = (recv[j, k, 0], recv[j, k, 1])
            if sign < 0:
                half = color_apply(wlink.at[to, mu], half, False)
            add_up(acc, half, mu, sign)
        return jnp.stack([a[0] for a in acc]), jnp.stack([a[1] for a in acc])

    def to_row(tiles):
        out = jnp.zeros((8, 128), jnp.float32)
        for k, tile in enumerate(tiles):
            for n in range(2):
                part = jnp.where(ev, tile, 0.0) if n == 0 else jnp.where(ev, 0.0, tile)
                out = jnp.where(row == 2 * k + n, jnp.sum(part, axis=0, keepdims=True), out)
        for by in (64, 32, 16):
            out = out + pltpu.roll(out, by, 1)
        return jnp.sum(jnp.where(lane >> 4 == row, out, 0.0), axis=0, keepdims=True)

    def from_row(line, k):
        return [
            jnp.sum(jnp.where(lane1 >> 4 == 2 * k + n, line, 0.0), axis=1, keepdims=True) for n in range(2)
        ]

    def row_send(group, slot, dst, stage):
        for k, offset in enumerate(group):
            pltpu.make_async_remote_copy(
                src_ref=row_s.at[slot, pl.ds(0, 1)], dst_ref=dst.at[pl.ds(k, 1)], send_sem=row_ssem.at[stage],
                recv_sem=row_rsem.at[stage], device_id=place(offset), device_id_type=MESH,
            ).start()

    def row_recv(slot, dst, stage):
        pltpu.make_async_copy(dst, dst, row_rsem.at[stage]).wait()
        return row_s[slot, 0:1, :] + jnp.sum(dst[...], axis=0, keepdims=True)

    first_r = (row_r0, row_r1, row_r2)

    def spread(pair):
        return jnp.where(ev, jnp.broadcast_to(pair[0], (8, 128)), jnp.broadcast_to(pair[1], (8, 128)))

    products = gamma_products()

    def project_loops(q, at_field, at_inner):
        for a in range(4):
            par_r, par_i = [], []
            for par, ref, at in ((0, field, at_field), (1, inner, at_inner)):
                br = bi = None
                for c in range(3):
                    sr, si = sfield[par, 0, a, c], sfield[par, 1, a, c]
                    pr, pi = ref[at, 0, :, c], ref[at, 1, :, c]
                    tr, ti = sr * pr + si * pi, sr * pi - si * pr
                    br, bi = (tr, ti) if br is None else (br + tr, bi + ti)
                par_r.append(br)
                par_i.append(bi)
            for re_im, (e, o) in enumerate((par_r, par_i)):
                bil[0, re_im, a] = jnp.where(ev, e, o)
                bil[1, re_im, a] = jnp.where(ev, o, e)

        def gammas(n, carry):
            for first in range(4):
                group = [g for g in range(16) if abs(products[g][0, first]) > 0.5]
                perm = [int(np.argmax(np.abs(products[group[0]][a]))) for a in range(4)]
                terms = [(bil[n, 0, a, perm[a]], bil[n, 1, a, perm[a]]) for a in range(4)]
                for g in group:
                    acc = None
                    for a in range(4):
                        power = int(round(np.angle(products[g][a, perm[a]]) / (math.pi / 2))) % 4
                        acc = times_i(power, *terms[a]) if acc is None else add_times_i(power, acc, terms[a])
                    for re_im in range(2):
                        start = pl.multiple_of((re_im * 32 + n * 16 + g) * 8, 8)
                        cur[pl.ds(start, 8), :] = acc[re_im]
            return carry

        lax.fori_loop(0, 2, gammas, 0)
        out = jnp.zeros((32, 128), jnp.float32)
        contract = (((1,), (1,)), ((), ()))
        for s in range(8):
            both = jnp.concatenate([cur[pl.ds(s, 32, stride=8), :], cur[pl.ds(256 + s, 32, stride=8), :]], axis=1)
            hi = both.astype(jnp.bfloat16)
            lo = (both - hi.astype(jnp.float32)).astype(jnp.bfloat16)
            wide = slice(s * 256, s * 256 + 256)
            ph, plo = phase_hi[:, wide], phase_lo[:, wide]
            main = lax.dot_general(jnp.concatenate([hi, lo], axis=0), ph, contract, preferred_element_type=jnp.float32)
            out = out + main[:32] + main[32:]
            out = out + lax.dot_general(hi, plo, contract, preferred_element_type=jnp.float32)
        loop_s[pl.ds(q, 32, stride=8), :] = out

    def loops_send():
        for k, offset in enumerate(ALONG_SPACE):
            target, _ = place(offset)
            pltpu.make_async_remote_copy(
                src_ref=loop_s.at[pl.ds(pl.multiple_of(target * 8, 8), 8)], dst_ref=loop_r.at[k],
                send_sem=loop_ssem, recv_sem=loop_rsem, device_id=(target, t), device_id_type=MESH,
            ).start()

    def nothing():
        pass

    def pair(p, carry):
        forward = p % 2
        g5 = 2.0 * forward - 1.0 if isinstance(p, int) else (2 * forward - 1).astype(jnp.float32)

        def flip(v):
            return jnp.concatenate([v[:2], v[2:] * g5], axis=0)

        def early_a():
            @when(p == 2)
            def _():
                row_send(ROUNDS[0], 0, first_r[0], 0)

            @when(p == 3)
            def _():
                row_send(ROUNDS[2], 2, first_r[2], 2)

        def late_a():
            @when(p == 0)
            def _():
                make_phases()

        def early_b():
            @when(p == 2)
            def _():
                row_s[1, 0:1, :] = row_recv(0, first_r[0], 0)
                row_send(ROUNDS[1], 1, first_r[1], 1)

        def late_b():
            cr, ci = clover_apply(wclov.at[forward, 0], field[p, 0], field[p, 1])
            base[0] = cr
            base[1] = ci

            @when(p == 3)
            def _():
                line = row_recv(2, first_r[2], 2)
                row_s[3, 0:1, :] = line
                rr, image = from_row(line, 0), from_row(line, 1)
                alpha = spread([rr[n] / image[n] for n in range(2)])
                alpha_ref[0] = alpha
                alpha_odd = spread([rr[1 - n] / image[1 - n] for n in range(2)])
                sq = None
                for re_im in range(2):
                    r = field[1, re_im] - alpha * field[3, re_im]
                    field[6, re_im] = r
                    inner[5, re_im] = inner[1, re_im] - alpha_odd * inner[3, re_im]
                    s = jnp.sum(r * r, axis=(0, 1))
                    sq = s if sq is None else sq + s
                alpha_ref[1] = sq

            @when(p > 0)
            def _():
                at_field = pick(p == 1, 5, pick(p == 2, 1, 6))
                at_inner = pick(p == 1, 4, pick(p == 2, 1, 5))
                project_loops(p - 1, at_field, at_inner)

            @when(p == 3)
            def _():
                loops_send()

        fr, fi = field[p, 0], field[p, 1]
        hr, hi = hop(2 * p + 1, 0, flip(fr), flip(fi), early_a, late_a)
        vr, vi = clover_apply(wclov.at[forward, 1], hr, hi)
        vr, vi = KAPPA * vr, KAPPA * vi
        inner[p, 0] = vr
        inner[p, 1] = vi
        hr, hi = hop(2 * p + 2, 1, vr, vi, early_b, late_b)
        outr, outi = base[0] - KAPPA * flip(hr), base[1] - KAPPA * flip(hi)
        field[p + 1, 0] = outr
        field[p + 1, 1] = outi

        @when(p == 1)
        def _():
            r0, r1 = field[1, 0], field[1, 1]
            i0, i1 = field[2, 0], field[2, 1]
            tiles = [jnp.sum(a * a + b * b, axis=(0, 1)) for a, b in ((r0, r1), (i0, i1))]
            row_s[0, 0:1, :] = to_row(tiles)

        @when(p == 2)
        def _():
            row_s[2, 0:1, :] = row_recv(1, first_r[1], 1)

        return carry

    loads[0].wait()
    for re_im in range(2):
        a = src[0, re_im]
        b = move(src[1, re_im], 2, -1)
        sfield[0, re_im] = jnp.where(ev, a, b)
        sfield[1, re_im] = jnp.where(ev, b, a)
    loads[1].wait()
    pack_clover(((1, 1),))
    cr, ci = clover_apply(wclov.at[1, 1], sfield[1, 0], sfield[1, 1])
    inner[4, 0] = cr
    inner[4, 1] = ci
    loads[2].wait()
    pack_links((0, 3))
    pl.semaphore_wait(barrier, len(greeted))
    hr, hi = hop(
        0, 1, cr, ci, lambda: pack_links((1, 2)), lambda: pack_clover(((0, 1), (0, 0), (1, 0)))
    )
    field[0, 0] = sfield[0, 0] + KAPPA * hr
    field[0, 1] = sfield[0, 1] + KAPPA * hi

    if UNROLL:
        for p in range(4):
            pair(p, 0)
    else:
        lax.fori_loop(0, 4, pair, 0)

    alpha = alpha_ref[0]
    m1 = m2 = None
    for re_im in range(2):
        v, w = field[2, re_im] - alpha * field[4, re_im], field[2, re_im]
        a, b = jnp.sum(v * v, axis=(0, 1)), jnp.sum(v * w, axis=(0, 1))
        m1, m2 = (a, b) if m1 is None else (m1 + a, m2 + b)
    row_s[4, 0:1, :] = to_row([alpha_ref[1], m1, m2])
    row_send(ALONG_Z, 4, last_r1, 3)
    second = x >= n_space // 2
    angle = momrow[0:1, :].astype(jnp.int32) * second.astype(jnp.int32)
    cos, sin = cos_sin(angle & 31)
    sin = jnp.where(lane1 < 64, -sin, sin)
    row_s[5, 0:1, :] = row_recv(4, last_r1, 3)
    row_send(ALONG_SPACE, 5, last_r2, 4)
    pltpu.make_async_copy(loop_r, loop_r, loop_rsem).wait()
    own = loop_s[pl.ds(pl.multiple_of(x * 8, 8), 8), :]
    piece = own + jnp.sum(loop_r[...], axis=0)
    piece = piece * cos + pltpu.roll(piece, 64, 1) * sin
    piece = piece * (1.0 / math.sqrt(n_space * NY * NZ))
    start = row_s[3, 0:1, :]
    rr0, im0 = [jnp.where(second, v[1], v[0]) for v in (from_row(start, 0), from_row(start, 1))]
    line = row_recv(5, last_r2, 4)
    rr1, m1, m2 = [jnp.where(second, v[1], v[0]) for v in (from_row(line, 0), from_row(line, 1), from_row(line, 2))]
    alpha0, beta = rr0 / im0, rr1 / rr0
    alpha1 = rr1 / (m1 + beta * (2.0 * m2 + beta * im0))
    line = piece[0:1] + (alpha0 + alpha1 * beta) * piece[1:2] + alpha1 * piece[2:3]
    out_ref[0] = line[:, 0:n_mom]
    out_ref[1] = line[:, 64 : 64 + n_mom]

    pltpu.make_async_copy(send, send, send_sem).wait()
    for stage, ref in enumerate((row_r0, row_r1, row_r2, last_r1, last_r2)):
        pltpu.make_async_copy(ref, ref, row_ssem.at[stage]).wait()
    pltpu.make_async_copy(loop_r, loop_r, loop_ssem).wait()


def solution(mesh):
    n_space, n_tm = mesh.shape["space"], mesh.shape["tm"]

    def local(sources, links, clover, momenta):
        f32 = jnp.float32
        n_mom = momenta.shape[0]
        tile = (8, 128)
        scratch = [
            pltpu.VMEM((2, 2, 4, 3) + tile, f32),
            pltpu.VMEM((2, 2, 6, 6) + tile, f32),
            pltpu.VMEM((4, 2, 3, 3) + tile, f32),
            pltpu.VMEM((3, n_mom), jnp.int32),
            pltpu.VMEM((2, 4, 2, 3, 3) + tile, f32),
            pltpu.VMEM((2, 2, 2, 2, 6, 6) + tile, f32),
            pltpu.VMEM((2, 2, 4, 3) + tile, f32),
            pltpu.VMEM((7, 2, 4, 3) + tile, f32),
            pltpu.VMEM((6, 2, 4, 3) + tile, f32),
            pltpu.VMEM((2, 4, 3) + tile, f32),
            pltpu.VMEM((2, 2, 4, 4) + tile, f32),
            pltpu.VMEM((512, 128), f32),
            pltpu.VMEM((128, 2048), jnp.bfloat16),
            pltpu.VMEM((128, 2048), jnp.bfloat16),
            pltpu.VMEM(tile, f32),
            pltpu.VMEM((9, 4, 2, 2, 3) + tile, f32),
            pltpu.VMEM((9, 4, 2, 2, 3) + tile, f32),
            pltpu.VMEM((6,) + tile, f32),
            *[pltpu.VMEM((len(group), 128), f32) for group in ROUNDS + (ALONG_Z, ALONG_SPACE)],
            pltpu.VMEM((2,) + tile, f32),
            pltpu.VMEM((256, 128), f32),
            pltpu.VMEM((n_space - 1,) + tile, f32),
            pltpu.SemaphoreType.DMA((4,)),
            pltpu.SemaphoreType.DMA,
            pltpu.SemaphoreType.DMA((9, 4)),
            pltpu.SemaphoreType.DMA((5,)),
            pltpu.SemaphoreType.DMA((5,)),
            pltpu.SemaphoreType.DMA,
            pltpu.SemaphoreType.DMA,
        ]
        out = pl.pallas_call(
            lambda *refs: kernel(n_space, n_tm, *refs),
            out_shape=jax.ShapeDtypeStruct((2, 1, n_mom), f32),
            in_specs=[pl.BlockSpec(memory_space=pl.ANY)] * 4,
            out_specs=pl.BlockSpec(memory_space=pltpu.VMEM),
            scratch_shapes=scratch,
            compiler_params=pltpu.CompilerParams(
                collective_id=0, has_side_effects=True, vmem_limit_bytes=60 * 1024 * 1024
            ),
            name="loops",
        )(
            sources.reshape((2, 2, 4, 3) + tile),
            clover.reshape((2, 2, 6, 6) + tile),
            links.reshape((4, 2, 3, 3) + tile),
            momenta.T,
        )
        return out.reshape(2, 1, n_mom, 1)

    placed = P(None, None, None, None, "space", "tm", None)
    return jax.shard_map(
        local, mesh=mesh, in_specs=(placed, placed, placed, P()), out_specs=P(None, "space", None, "tm"), check_vma=False
    )
```

```python
import math

import jax
import jax.numpy as jnp
import numpy as np
from jax import lax
from jax.experimental import pallas as pl
from jax.experimental.pallas import tpu as pltpu
from jax.sharding import PartitionSpec as P

MESH = pl.DeviceIdType.MESH
NZ = 32
NY = 32
KAPPA = 0.1
MOM = 48
UNROLL = True


UPPER = (((1, 1), (0, 1)), ((1, 0), (0, 2)), ((0, 1), (1, 3)), ((0, 0), (1, 0)))
LOWER = (((1, 3), (0, 3)), ((1, 2), (0, 0)), ((0, 3), (1, 1)), ((0, 0), (1, 0)))


def gamma_products():
    sigma = [
        np.array([[0, 1], [1, 0]]) + 0j,
        np.array([[0, -1j], [1j, 0]]),
        np.array([[1, 0], [0, -1]]) + 0j,
    ]
    zero = np.zeros((2, 2)) + 0j
    singles = [np.block([[zero, 1j * s], [-1j * s, zero]]) for s in sigma]
    singles.append(np.block([[zero, np.eye(2)], [np.eye(2), zero]]) + 0j)
    products = []
    for bits in range(16):
        product = np.eye(4) + 0j
        for direction in range(4):
            if bits >> direction & 1:
                product = product @ singles[direction]
        products.append(product)
    return products


def times_i(power, re, im):
    power %= 4
    if power == 0:
        return re, im
    if power == 1:
        return -im, re
    if power == 2:
        return -re, -im
    return im, -re


def add_times_i(power, acc, term):
    (ar, ai), (re, im) = acc, term
    power %= 4
    if power == 0:
        return ar + re, ai + im
    if power == 1:
        return ar - im, ai + re
    if power == 2:
        return ar - re, ai - im
    return ar + im, ai - re


def color_apply(link, half, adjoint):
    hr, hi = half
    outr = outi = None
    for b in range(3):
        if adjoint:
            ur, ui = link[0, b], link[1, b]
        else:
            ur, ui = link[0, :, b], link[1, :, b]
        ur, ui = ur[None], ui[None]
        xr, xi = hr[:, b][:, None], hi[:, b][:, None]
        if adjoint:
            tr, ti = ur * xr + ui * xi, ur * xi - ui * xr
        else:
            tr, ti = ur * xr - ui * xi, ur * xi + ui * xr
        outr, outi = (tr, ti) if outr is None else (outr + tr, outi + ti)
    return outr, outi


def clover_apply(mat, fr, fi):
    xr, xi = fr.reshape(2, 6, 8, 128), fi.reshape(2, 6, 8, 128)
    outr = outi = None
    for i in range(6):
        cr, ci = mat[0, :, :, i], mat[1, :, :, i]
        vr, vi = xr[:, i][:, None], xi[:, i][:, None]
        tr, ti = cr * vr - ci * vi, cr * vi + ci * vr
        outr, outi = (tr, ti) if outr is None else (outr + tr, outi + ti)
    return outr.reshape(4, 3, 8, 128), outi.reshape(4, 3, 8, 128)


def fan(ys, xs, cores, zs):
    offsets = [(y, x, c, z) for y in ys for x in xs for c in cores for z in zs if (y, x, c, z) != (0, 0, 0, 0)]
    return sorted(offsets, key=lambda o: -(min(o[0], 4 - o[0]) + min(o[1], 4 - o[1]) + min(o[3], 4 - o[3])))


ALONG_ROW = fan([0], range(4), range(2), [0])
ALONG_Y = fan(range(4), [0], [0], [0])
ALONG_Z = fan([0], [0], [0], range(4))
ALONG_SPACE = fan(range(4), range(4), range(2), [0])
EVERYONE = fan(range(4), range(4), range(2), range(4))
ROUNDS = (ALONG_ROW, ALONG_Y, ALONG_Z)


def when(condition):
    if isinstance(condition, bool):
        return (lambda f: f()) if condition else (lambda f: None)
    return pl.when(condition)


def pick(condition, a, b):
    if isinstance(condition, bool):
        return a if condition else b
    return jnp.where(condition, a, b)


def kernel(
    n_space, n_tm,
    src_hbm, clov_hbm, link_hbm, mom_hbm, out_ref,
    src, clov, link, mom_ref, wlink, wclov, sfield, field, inner, base, bil, cur, phase_hi, phase_lo, momrow,
    send, recv, row_s, row_r0, row_r1, row_r2, last_r, alpha_ref, loop_s, loop_r,
    in_sem, send_sem, recv_sem, row_ssem, row_rsem, loop_ssem, loop_rsem,
):
    x = lax.axis_index("space")
    t = lax.axis_index("tm")
    x_up, x_dn = lax.rem(x + 1, n_space), lax.rem(x + n_space - 1, n_space)
    t_up, t_dn = lax.rem(t + 1, n_tm), lax.rem(t + n_tm - 1, n_tm)

    loads = [
        pltpu.make_async_copy(a, b, in_sem.at[k])
        for k, (a, b) in enumerate(((src_hbm, src), (link_hbm, link), (clov_hbm, clov), (mom_hbm, mom_ref)))
    ]
    for load in loads:
        load.start()

    def space_at(dy, dx, dc):
        return ((x // 8 + dy) & 3) * 8 + (((x // 2) + dx) & 3) * 2 + ((x + dc) & 1)

    def place(offset):
        dy, dx, dc, dz = offset
        return (space_at(dy, dx, dc), (t + dz) & 3)

    barrier = pltpu.get_barrier_semaphore()
    greeted = [(x_up, t), (x_dn, t)] + [place(offset) for group in ROUNDS for offset in group]
    for device in greeted:
        pl.semaphore_signal(barrier, inc=1, device_id=device, device_id_type=MESH)

    lane = lax.broadcasted_iota(jnp.int32, (8, 128), 1)
    row = lax.broadcasted_iota(jnp.int32, (8, 128), 0)
    lane1 = lax.broadcasted_iota(jnp.int32, (1, 128), 1)
    zc = lane & 31
    yc = row * 4 + (lane >> 5)
    ev = ((yc + zc + x + t) & 1) == 0

    def move(v, axis, by):
        last = v.ndim - 1
        if axis == 2:
            if by == 1:
                return jnp.where(zc == 31, pltpu.roll(v, 31, last), pltpu.roll(v, 127, last))
            return jnp.where(zc == 0, pltpu.roll(v, 97, last), pltpu.roll(v, 1, last))
        if by == 1:
            a = pltpu.roll(v, 96, last)
            return jnp.where(lane >= 96, pltpu.roll(a, 7, last - 1), a)
        a = pltpu.roll(v, 32, last)
        return jnp.where(lane < 32, pltpu.roll(a, 1, last - 1), a)

    def cos_sin(k):
        a = (k - 16).astype(jnp.float32) * (math.pi / 32)
        q = a * a
        s = 1.0 / math.factorial(11)
        for m in (9, 7, 5, 3, 1):
            s = 1.0 / math.factorial(m) - q * s
        s = s * a
        c = 1.0 / math.factorial(12)
        for m in (10, 8, 6, 4, 2, 0):
            c = 1.0 / math.factorial(m) - q * c
        return 2.0 * s * s - 1.0, -2.0 * s * c

    def pack_clover(entries):
        def step(k, carry):
            re_im, chi, r = k // 12, (k // 6) % 2, k % 6
            sign = (1 - 2 * re_im).astype(jnp.float32)
            a = clov[re_im, chi, r]
            b = move(a, 2, -1)
            for forward, par in entries:
                v = jnp.where(ev, a, b) if par == 0 else jnp.where(ev, b, a)
                if forward:
                    wclov[1, par, re_im, chi, r] = v
                else:
                    wclov[0, par, re_im, chi, :, r] = v * sign
            return carry

        lax.fori_loop(0, 24, step, 0)

    t_sign = jnp.where(t == n_tm - 1, -1.0, 1.0).astype(jnp.float32)

    def pack_links(directions):
        for mu in directions:
            for re_im in range(2):
                a = link[mu, re_im]
                if mu == 3:
                    a = a * t_sign
                b = move(a, 2, -1)
                wlink[0, mu, re_im] = jnp.where(ev, a, b)
                wlink[1, mu, re_im] = jnp.where(ev, b, a)

    n_mom = mom_ref.shape[1]

    def make_phases():
        loads[3].wait()
        mom = mom_ref[...].astype(jnp.float32)
        eye = lax.broadcasted_iota(jnp.int32, (MOM, n_mom), 0) == lax.broadcasted_iota(jnp.int32, (MOM, n_mom), 1)
        columns = [
            jnp.sum(jnp.where(eye, jnp.broadcast_to(mom[k : k + 1], (MOM, n_mom)), 0.0), axis=1, keepdims=True).astype(jnp.int32)
            for k in range(3)
        ]
        zero_rows = jnp.zeros((64 - MOM, 2048), jnp.bfloat16)
        for ref in (phase_hi, phase_lo):
            ref[MOM:64, :] = zero_rows
            ref[64 + MOM : 128, :] = zero_rows

        def phases(s, carry):
            yrow = s * 4 + (lane1 >> 5)
            zrow = lane1 & 31
            c, sn = cos_sin((columns[0] * x + columns[1] * yrow + columns[2] * zrow) & 31)
            for value, places in ((c, ((0, 0, 1), (64, 128, 1))), (sn, ((0, 128, 1), (64, 0, -1)))):
                hi = value.astype(jnp.bfloat16)
                lo = (value - hi.astype(jnp.float32)).astype(jnp.bfloat16)
                for r0, c0, sign in places:
                    at = pl.ds(pl.multiple_of(s * 256 + c0, 128), 128)
                    phase_hi[r0 : r0 + MOM, at] = hi * sign
                    phase_lo[r0 : r0 + MOM, at] = lo * sign
            return carry

        lax.fori_loop(0, 8, phases, 0)
        momrow[...] = jnp.zeros_like(momrow)
        momrow[0:1, 0:n_mom] = mom[2:3]
        momrow[0:1, 64 : 64 + n_mom] = mom[2:3]
        loop_s[...] = jnp.zeros_like(loop_s)
        zero = jnp.zeros((4, 3, 8, 128), jnp.float32)
        field[5, 0] = zero
        field[5, 1] = zero

    ROUTES = ((0, -1, (x_dn, t)), (0, 1, (x_up, t)), (3, -1, (x, t_dn)), (3, 1, (x, t_up)))

    def halo(j, k):
        return pltpu.make_async_remote_copy(
            src_ref=send.at[j, k], dst_ref=recv.at[j, k], send_sem=send_sem, recv_sem=recv_sem.at[j, k],
            device_id=ROUTES[k][2], device_id_type=MESH,
        )

    def project(fr, fi, mu, sign):
        rows_r, rows_i = [], []
        for spin in range(2):
            col, power = UPPER[mu][spin]
            if sign < 0:
                power += 2
            r, i = add_times_i(power, (fr[spin], fi[spin]), (fr[2 + col], fi[2 + col]))
            rows_r.append(r)
            rows_i.append(i)
        return jnp.stack(rows_r), jnp.stack(rows_i)

    def add_up(acc, half, mu, sign):
        hr, hi = half
        for spin in range(2):
            acc[spin] = (hr[spin], hi[spin]) if acc[spin] is None else (acc[spin][0] + hr[spin], acc[spin][1] + hi[spin])
            col, power = LOWER[mu][spin]
            if sign < 0:
                power += 2
            term = (hr[col], hi[col])
            acc[2 + spin] = times_i(power, *term) if acc[2 + spin] is None else add_times_i(power, acc[2 + spin], term)

    def hop(j, par, fr, fi, early, late):
        to = 1 - par
        for k, (mu, sign, _) in enumerate(ROUTES):
            half = project(fr, fi, mu, sign)
            if sign > 0:
                half = color_apply(wlink.at[par, mu], half, True)
            send[j, k, 0] = half[0]
            send[j, k, 1] = half[1]
            halo(j, k).start()
        early()
        acc = [None] * 4
        for mu in (1, 2):
            hr, hi = project(fr, fi, mu, -1)
            ahead = (move(hr, mu, 1), move(hi, mu, 1))
            add_up(acc, color_apply(wlink.at[to, mu], ahead, False), mu, -1)
            hr, hi = color_apply(wlink.at[par, mu], project(fr, fi, mu, 1), True)
            add_up(acc, (move(hr, mu, -1), move(hi, mu, -1)), mu, 1)
        late()
        for k in (2, 3, 0, 1):
            mu, sign, _ = ROUTES[k]
            halo(j, k).wait_recv()
            half = (recv[j, k, 0], recv[j, k, 1])
            if sign < 0:
                half = color_apply(wlink.at[to, mu], half, False)
            add_up(acc, half, mu, sign)
        return jnp.stack([a[0] for a in acc]), jnp.stack([a[1] for a in acc])

    def to_row(tiles):
        out = jnp.zeros((8, 128), jnp.float32)
        for k, tile in enumerate(tiles):
            for n in range(2):
                part = jnp.where(ev, tile, 0.0) if n == 0 else jnp.where(ev, 0.0, tile)
                out = jnp.where(row == 2 * k + n, jnp.sum(part, axis=0, keepdims=True), out)
        for by in (64, 32, 16):
            out = out + pltpu.roll(out, by, 1)
        return jnp.sum(jnp.where(lane >> 4 == row, out, 0.0), axis=0, keepdims=True)

    def from_row(line, k):
        return [
            jnp.sum(jnp.where(lane1 >> 4 == 2 * k + n, line, 0.0), axis=1, keepdims=True) for n in range(2)
        ]

    def row_send(group, slot, dst, stage):
        for k, offset in enumerate(group):
            pltpu.make_async_remote_copy(
                src_ref=row_s.at[slot, pl.ds(0, 1)], dst_ref=dst.at[pl.ds(k, 1)], send_sem=row_ssem.at[stage],
                recv_sem=row_rsem.at[stage], device_id=place(offset), device_id_type=MESH,
            ).start()

    def row_recv(slot, dst, stage):
        pltpu.make_async_copy(dst, dst, row_rsem.at[stage]).wait()
        return row_s[slot, 0:1, :] + jnp.sum(dst[...], axis=0, keepdims=True)

    first_r = (row_r0, row_r1, row_r2)

    def spread(pair):
        return jnp.where(ev, jnp.broadcast_to(pair[0], (8, 128)), jnp.broadcast_to(pair[1], (8, 128)))

    products = gamma_products()

    def project_loops(q, at_field, at_inner):
        for a in range(4):
            par_r, par_i = [], []
            for par, ref, at in ((0, field, at_field), (1, inner, at_inner)):
                br = bi = None
                for c in range(3):
                    sr, si = sfield[par, 0, a, c], sfield[par, 1, a, c]
                    pr, pi = ref[at, 0, :, c], ref[at, 1, :, c]
                    tr, ti = sr * pr + si * pi, sr * pi - si * pr
                    br, bi = (tr, ti) if br is None else (br + tr, bi + ti)
                par_r.append(br)
                par_i.append(bi)
            for re_im, (e, o) in enumerate((par_r, par_i)):
                bil[0, re_im, a] = jnp.where(ev, e, o)
                bil[1, re_im, a] = jnp.where(ev, o, e)

        def gammas(n, carry):
            for first in range(4):
                group = [g for g in range(16) if abs(products[g][0, first]) > 0.5]
                perm = [int(np.argmax(np.abs(products[group[0]][a]))) for a in range(4)]
                terms = [(bil[n, 0, a, perm[a]], bil[n, 1, a, perm[a]]) for a in range(4)]
                for g in group:
                    acc = None
                    for a in range(4):
                        power = int(round(np.angle(products[g][a, perm[a]]) / (math.pi / 2))) % 4
                        acc = times_i(power, *terms[a]) if acc is None else add_times_i(power, acc, terms[a])
                    for re_im in range(2):
                        start = pl.multiple_of((re_im * 32 + n * 16 + g) * 8, 8)
                        cur[pl.ds(start, 8), :] = acc[re_im]
            return carry

        lax.fori_loop(0, 2, gammas, 0)
        out = jnp.zeros((32, 128), jnp.float32)
        contract = (((1,), (1,)), ((), ()))
        for s in range(8):
            both = jnp.concatenate([cur[pl.ds(s, 32, stride=8), :], cur[pl.ds(256 + s, 32, stride=8), :]], axis=1)
            hi = both.astype(jnp.bfloat16)
            lo = (both - hi.astype(jnp.float32)).astype(jnp.bfloat16)
            wide = slice(s * 256, s * 256 + 256)
            ph, plo = phase_hi[:, wide], phase_lo[:, wide]
            main = lax.dot_general(jnp.concatenate([hi, lo], axis=0), ph, contract, preferred_element_type=jnp.float32)
            out = out + main[:32] + main[32:]
            out = out + lax.dot_general(hi, plo, contract, preferred_element_type=jnp.float32)
        loop_s[pl.ds(q, 32, stride=8), :] = out

    def loops_send():
        for k, offset in enumerate(ALONG_SPACE):
            target, _ = place(offset)
            pltpu.make_async_remote_copy(
                src_ref=loop_s.at[pl.ds(pl.multiple_of(target * 8, 8), 8)], dst_ref=loop_r.at[k],
                send_sem=loop_ssem, recv_sem=loop_rsem, device_id=(target, t), device_id_type=MESH,
            ).start()

    def nothing():
        pass

    def pair(p, carry):
        forward = p % 2
        g5 = 2.0 * forward - 1.0 if isinstance(p, int) else (2 * forward - 1).astype(jnp.float32)

        def flip(v):
            return jnp.concatenate([v[:2], v[2:] * g5], axis=0)

        def early_a():
            @when(p == 2)
            def _():
                row_send(ROUNDS[0], 0, first_r[0], 0)

            @when(p == 3)
            def _():
                row_send(ROUNDS[2], 2, first_r[2], 2)

        def late_a():
            @when(p == 0)
            def _():
                make_phases()

        def early_b():
            @when(p == 2)
            def _():
                row_s[1, 0:1, :] = row_recv(0, first_r[0], 0)
                row_send(ROUNDS[1], 1, first_r[1], 1)

        def late_b():
            cr, ci = clover_apply(wclov.at[forward, 0], field[p, 0], field[p, 1])
            base[0] = cr
            base[1] = ci

            @when(p == 3)
            def _():
                line = row_recv(2, first_r[2], 2)
                row_s[3, 0:1, :] = line
                rr, image = from_row(line, 0), from_row(line, 1)
                alpha = spread([rr[n] / image[n] for n in range(2)])
                alpha_ref[0] = alpha
                alpha_odd = spread([rr[1 - n] / image[1 - n] for n in range(2)])
                sq = None
                for re_im in range(2):
                    r = field[1, re_im] - alpha * field[3, re_im]
                    field[6, re_im] = r
                    inner[5, re_im] = inner[1, re_im] - alpha_odd * inner[3, re_im]
                    s = jnp.sum(r * r, axis=(0, 1))
                    sq = s if sq is None else sq + s
                alpha_ref[1] = sq

            @when(p > 0)
            def _():
                at_field = pick(p == 1, 5, pick(p == 2, 1, 6))
                at_inner = pick(p == 1, 4, pick(p == 2, 1, 5))
                project_loops(p - 1, at_field, at_inner)

            @when(p == 3)
            def _():
                loops_send()

        fr, fi = field[p, 0], field[p, 1]
        hr, hi = hop(2 * p + 1, 0, flip(fr), flip(fi), early_a, late_a)
        vr, vi = clover_apply(wclov.at[forward, 1], hr, hi)
        vr, vi = KAPPA * vr, KAPPA * vi
        inner[p, 0] = vr
        inner[p, 1] = vi
        hr, hi = hop(2 * p + 2, 1, vr, vi, early_b, late_b)
        outr, outi = base[0] - KAPPA * flip(hr), base[1] - KAPPA * flip(hi)
        field[p + 1, 0] = outr
        field[p + 1, 1] = outi

        @when(p == 1)
        def _():
            r0, r1 = field[1, 0], field[1, 1]
            i0, i1 = field[2, 0], field[2, 1]
            tiles = [jnp.sum(a * a + b * b, axis=(0, 1)) for a, b in ((r0, r1), (i0, i1))]
            row_s[0, 0:1, :] = to_row(tiles)

        @when(p == 2)
        def _():
            row_s[2, 0:1, :] = row_recv(1, first_r[1], 1)

        return carry

    loads[0].wait()
    for re_im in range(2):
        a = src[0, re_im]
        b = move(src[1, re_im], 2, -1)
        sfield[0, re_im] = jnp.where(ev, a, b)
        sfield[1, re_im] = jnp.where(ev, b, a)
    loads[1].wait()
    pack_links((0, 3))
    loads[2].wait()
    pack_clover(((1, 1),))
    cr, ci = clover_apply(wclov.at[1, 1], sfield[1, 0], sfield[1, 1])
    inner[4, 0] = cr
    inner[4, 1] = ci
    pl.semaphore_wait(barrier, len(greeted))
    hr, hi = hop(
        0, 1, cr, ci, lambda: pack_links((1, 2)), lambda: pack_clover(((0, 1), (0, 0), (1, 0)))
    )
    field[0, 0] = sfield[0, 0] + KAPPA * hr
    field[0, 1] = sfield[0, 1] + KAPPA * hi

    if UNROLL:
        for p in range(4):
            pair(p, 0)
    else:
        lax.fori_loop(0, 4, pair, 0)

    alpha = alpha_ref[0]
    m1 = m2 = None
    for re_im in range(2):
        v, w = field[2, re_im] - alpha * field[4, re_im], field[2, re_im]
        a, b = jnp.sum(v * v, axis=(0, 1)), jnp.sum(v * w, axis=(0, 1))
        m1, m2 = (a, b) if m1 is None else (m1 + a, m2 + b)
    row_s[4, 0:1, :] = to_row([alpha_ref[1], m1, m2])
    row_send(EVERYONE, 4, last_r, 3)
    second = x >= n_space // 2
    angle = momrow[0:1, :].astype(jnp.int32) * second.astype(jnp.int32)
    cos, sin = cos_sin(angle & 31)
    sin = jnp.where(lane1 < 64, -sin, sin)
    pltpu.make_async_copy(loop_r, loop_r, loop_rsem).wait()
    own = loop_s[pl.ds(pl.multiple_of(x * 8, 8), 8), :]
    piece = own + jnp.sum(loop_r[...], axis=0)
    piece = piece * cos + pltpu.roll(piece, 64, 1) * sin
    piece = piece * (1.0 / math.sqrt(n_space * NY * NZ))
    start = row_s[3, 0:1, :]
    rr0, im0 = [jnp.where(second, v[1], v[0]) for v in (from_row(start, 0), from_row(start, 1))]
    line = row_recv(4, last_r, 3)
    rr1, m1, m2 = [jnp.where(second, v[1], v[0]) for v in (from_row(line, 0), from_row(line, 1), from_row(line, 2))]
    alpha0, beta = rr0 / im0, rr1 / rr0
    alpha1 = rr1 / (m1 + beta * (2.0 * m2 + beta * im0))
    line = piece[0:1] + (alpha0 + alpha1 * beta) * piece[1:2] + alpha1 * piece[2:3]
    out_ref[0] = line[:, 0:n_mom]
    out_ref[1] = line[:, 64 : 64 + n_mom]

    pltpu.make_async_copy(send, send, send_sem).wait()
    for stage, ref in enumerate((row_r0, row_r1, row_r2, last_r)):
        pltpu.make_async_copy(ref, ref, row_ssem.at[stage]).wait()
    pltpu.make_async_copy(loop_r, loop_r, loop_ssem).wait()


def solution(mesh):
    n_space, n_tm = mesh.shape["space"], mesh.shape["tm"]

    def local(sources, links, clover, momenta):
        f32 = jnp.float32
        n_mom = momenta.shape[0]
        tile = (8, 128)
        scratch = [
            pltpu.VMEM((2, 2, 4, 3) + tile, f32),
            pltpu.VMEM((2, 2, 6, 6) + tile, f32),
            pltpu.VMEM((4, 2, 3, 3) + tile, f32),
            pltpu.VMEM((3, n_mom), jnp.int32),
            pltpu.VMEM((2, 4, 2, 3, 3) + tile, f32),
            pltpu.VMEM((2, 2, 2, 2, 6, 6) + tile, f32),
            pltpu.VMEM((2, 2, 4, 3) + tile, f32),
            pltpu.VMEM((7, 2, 4, 3) + tile, f32),
            pltpu.VMEM((6, 2, 4, 3) + tile, f32),
            pltpu.VMEM((2, 4, 3) + tile, f32),
            pltpu.VMEM((2, 2, 4, 4) + tile, f32),
            pltpu.VMEM((512, 128), f32),
            pltpu.VMEM((128, 2048), jnp.bfloat16),
            pltpu.VMEM((128, 2048), jnp.bfloat16),
            pltpu.VMEM(tile, f32),
            pltpu.VMEM((9, 4, 2, 2, 3) + tile, f32),
            pltpu.VMEM((9, 4, 2, 2, 3) + tile, f32),
            pltpu.VMEM((6,) + tile, f32),
            *[pltpu.VMEM((len(group), 128), f32) for group in ROUNDS + (EVERYONE,)],
            pltpu.VMEM((2,) + tile, f32),
            pltpu.VMEM((256, 128), f32),
            pltpu.VMEM((n_space - 1,) + tile, f32),
            pltpu.SemaphoreType.DMA((4,)),
            pltpu.SemaphoreType.DMA,
            pltpu.SemaphoreType.DMA((9, 4)),
            pltpu.SemaphoreType.DMA((5,)),
            pltpu.SemaphoreType.DMA((5,)),
            pltpu.SemaphoreType.DMA,
            pltpu.SemaphoreType.DMA,
        ]
        out = pl.pallas_call(
            lambda *refs: kernel(n_space, n_tm, *refs),
            out_shape=jax.ShapeDtypeStruct((2, 1, n_mom), f32),
            in_specs=[pl.BlockSpec(memory_space=pl.ANY)] * 4,
            out_specs=pl.BlockSpec(memory_space=pltpu.VMEM),
            scratch_shapes=scratch,
            compiler_params=pltpu.CompilerParams(
                collective_id=0, has_side_effects=True, vmem_limit_bytes=48 * 1024 * 1024
            ),
            name="loops",
        )(
            *[
                pltpu.with_memory_space_constraint(v, pltpu.HBM)
                for v in (
                    sources.reshape((2, 2, 4, 3) + tile),
                    clover.reshape((2, 2, 6, 6) + tile),
                    links.reshape((4, 2, 3, 3) + tile),
                    momenta.T,
                )
            ]
        )
        return out.reshape(2, 1, n_mom, 1)

    placed = P(None, None, None, None, "space", "tm", None)
    return jax.shard_map(
        local, mesh=mesh, in_specs=(placed, placed, placed, P()), out_specs=P(None, "space", None, "tm"), check_vma=False
    )
```

```python
import math

import jax
import jax.numpy as jnp
import numpy as np
from jax import lax
from jax.experimental import pallas as pl
from jax.experimental.pallas import tpu as pltpu
from jax.sharding import PartitionSpec as P

MESH = pl.DeviceIdType.MESH
NZ = 32
NY = 32
KAPPA = 0.1
MOM = 48


UPPER = (((1, 1), (0, 1)), ((1, 0), (0, 2)), ((0, 1), (1, 3)), ((0, 0), (1, 0)))
LOWER = (((1, 3), (0, 3)), ((1, 2), (0, 0)), ((0, 3), (1, 1)), ((0, 0), (1, 0)))


def gamma_products():
    sigma = [
        np.array([[0, 1], [1, 0]]) + 0j,
        np.array([[0, -1j], [1j, 0]]),
        np.array([[1, 0], [0, -1]]) + 0j,
    ]
    zero = np.zeros((2, 2)) + 0j
    singles = [np.block([[zero, 1j * s], [-1j * s, zero]]) for s in sigma]
    singles.append(np.block([[zero, np.eye(2)], [np.eye(2), zero]]) + 0j)
    products = []
    for bits in range(16):
        product = np.eye(4) + 0j
        for direction in range(4):
            if bits >> direction & 1:
                product = product @ singles[direction]
        products.append(product)
    return products


def times_i(power, re, im):
    power %= 4
    if power == 0:
        return re, im
    if power == 1:
        return -im, re
    if power == 2:
        return -re, -im
    return im, -re


def add_times_i(power, acc, term):
    (ar, ai), (re, im) = acc, term
    power %= 4
    if power == 0:
        return ar + re, ai + im
    if power == 1:
        return ar - im, ai + re
    if power == 2:
        return ar - re, ai - im
    return ar + im, ai - re


def color_apply(link, half, adjoint):
    hr, hi = half
    outr = outi = None
    for b in range(3):
        if adjoint:
            ur, ui = link[0, b], link[1, b]
        else:
            ur, ui = link[0, :, b], link[1, :, b]
        ur, ui = ur[None], ui[None]
        xr, xi = hr[:, b][:, None], hi[:, b][:, None]
        if adjoint:
            tr, ti = ur * xr + ui * xi, ur * xi - ui * xr
        else:
            tr, ti = ur * xr - ui * xi, ur * xi + ui * xr
        outr, outi = (tr, ti) if outr is None else (outr + tr, outi + ti)
    return outr, outi


def clover_apply(mat, fr, fi, adjoint):
    xr, xi = fr.reshape(2, 6, 8, 128), fi.reshape(2, 6, 8, 128)
    outr = outi = None
    for i in range(6):
        vr, vi = xr[:, i][:, None], xi[:, i][:, None]
        if adjoint:
            cr, ci = mat[0, :, i], mat[1, :, i]
            tr, ti = cr * vr + ci * vi, cr * vi - ci * vr
        else:
            cr, ci = mat[0, :, :, i], mat[1, :, :, i]
            tr, ti = cr * vr - ci * vi, cr * vi + ci * vr
        outr, outi = (tr, ti) if outr is None else (outr + tr, outi + ti)
    return outr.reshape(4, 3, 8, 128), outi.reshape(4, 3, 8, 128)


def flip(v):
    return jnp.concatenate([v[:2], -v[2:]], axis=0)


def fan(ys, xs, cores, zs):
    offsets = [(y, x, c, z) for y in ys for x in xs for c in cores for z in zs if (y, x, c, z) != (0, 0, 0, 0)]
    return sorted(offsets, key=lambda o: -(min(o[0], 4 - o[0]) + min(o[1], 4 - o[1]) + min(o[3], 4 - o[3])))


ALONG_ROW = fan([0], range(4), range(2), [0])
ALONG_Y = fan(range(4), [0], [0], [0])
ALONG_Z = fan([0], [0], [0], range(4))
ALONG_SPACE = fan(range(4), range(4), range(2), [0])
EVERYONE = fan(range(4), range(4), range(2), range(4))
ROUNDS = (ALONG_ROW, ALONG_Y, ALONG_Z)


def kernel(
    n_space, n_tm,
    src_hbm, clov_hbm, link_hbm, mom_hbm, out_ref,
    src, clov, link, mom_ref, wlink, wclov, sfield, field, inner, base, bil, cur, phase_hi, phase_lo, momrow,
    send, recv, row_s, row_r0, row_r1, row_r2, last_r, alpha_ref, loop_s, loop_r, far_clov, far_link, far_send, far_recv, far_raw, echo,
    in_sem, send_sem, recv_sem, row_ssem, row_rsem, loop_ssem, loop_rsem, far_ssem, far_rsem,
):
    x = lax.axis_index("space")
    t = lax.axis_index("tm")
    x_up, x_dn = lax.rem(x + 1, n_space), lax.rem(x + n_space - 1, n_space)
    t_up, t_dn = lax.rem(t + 1, n_tm), lax.rem(t + n_tm - 1, n_tm)

    loads = [
        pltpu.make_async_copy(a, b, in_sem.at[k])
        for k, (a, b) in enumerate(((src_hbm, src), (link_hbm, link), (clov_hbm, clov), (mom_hbm, mom_ref)))
    ]
    for load in loads:
        load.start()

    def space_at(dy, dx, dc):
        return ((x // 8 + dy) & 3) * 8 + (((x // 2) + dx) & 3) * 2 + ((x + dc) & 1)

    def place(offset):
        dy, dx, dc, dz = offset
        return (space_at(dy, dx, dc), (t + dz) & 3)

    barrier = pltpu.get_barrier_semaphore()
    greeted = [(x_up, t), (x_dn, t)] + [place(offset) for group in ROUNDS for offset in group]
    for device in greeted:
        pl.semaphore_signal(barrier, inc=1, device_id=device, device_id_type=MESH)

    lane = lax.broadcasted_iota(jnp.int32, (8, 128), 1)
    row = lax.broadcasted_iota(jnp.int32, (8, 128), 0)
    lane1 = lax.broadcasted_iota(jnp.int32, (1, 128), 1)
    zc = lane & 31
    yc = row * 4 + (lane >> 5)
    ev = ((yc + zc + x + t) & 1) == 0

    def move(v, axis, by):
        last = v.ndim - 1
        if axis == 2:
            if by == 1:
                return jnp.where(zc == 31, pltpu.roll(v, 31, last), pltpu.roll(v, 127, last))
            return jnp.where(zc == 0, pltpu.roll(v, 97, last), pltpu.roll(v, 1, last))
        if by == 1:
            a = pltpu.roll(v, 96, last)
            return jnp.where(lane >= 96, pltpu.roll(a, 7, last - 1), a)
        a = pltpu.roll(v, 32, last)
        return jnp.where(lane < 32, pltpu.roll(a, 1, last - 1), a)

    def cos_sin(k):
        a = (k - 16).astype(jnp.float32) * (math.pi / 32)
        q = a * a
        s = 1.0 / math.factorial(11)
        for m in (9, 7, 5, 3, 1):
            s = 1.0 / math.factorial(m) - q * s
        s = s * a
        c = 1.0 / math.factorial(12)
        for m in (10, 8, 6, 4, 2, 0):
            c = 1.0 / math.factorial(m) - q * c
        return 2.0 * s * s - 1.0, -2.0 * s * c

    def pack_clover(par):
        def step(k, carry):
            re_im, chi, r = k // 12, (k // 6) % 2, k % 6
            a = clov[re_im, chi, r]
            b = move(a, 2, -1)
            wclov[par, re_im, chi, r] = jnp.where(ev, a, b) if par == 0 else jnp.where(ev, b, a)
            return carry

        lax.fori_loop(0, 24, step, 0)

    t_sign = jnp.where(t == n_tm - 1, -1.0, 1.0).astype(jnp.float32)

    def pack_links(directions):
        for mu in directions:
            for re_im in range(2):
                a = link[mu, re_im]
                if mu == 3:
                    a = a * t_sign
                b = move(a, 2, -1)
                wlink[0, mu, re_im] = jnp.where(ev, a, b)
                wlink[1, mu, re_im] = jnp.where(ev, b, a)

    n_mom = mom_ref.shape[1]

    def make_phases():
        loads[3].wait()
        mom = mom_ref[...].astype(jnp.float32)
        eye = lax.broadcasted_iota(jnp.int32, (MOM, n_mom), 0) == lax.broadcasted_iota(jnp.int32, (MOM, n_mom), 1)
        columns = [
            jnp.sum(jnp.where(eye, jnp.broadcast_to(mom[k : k + 1], (MOM, n_mom)), 0.0), axis=1, keepdims=True).astype(jnp.int32)
            for k in range(3)
        ]
        zero_rows = jnp.zeros((64 - MOM, 2048), jnp.bfloat16)
        for ref in (phase_hi, phase_lo):
            ref[MOM:64, :] = zero_rows
            ref[64 + MOM : 128, :] = zero_rows

        def phases(s, carry):
            yrow = s * 4 + (lane1 >> 5)
            zrow = lane1 & 31
            c, sn = cos_sin((columns[0] * x + columns[1] * yrow + columns[2] * zrow) & 31)
            for value, places in ((c, ((0, 0, 1), (64, 128, 1))), (sn, ((0, 128, 1), (64, 0, -1)))):
                hi = value.astype(jnp.bfloat16)
                lo = (value - hi.astype(jnp.float32)).astype(jnp.bfloat16)
                for r0, c0, sign in places:
                    at = pl.ds(pl.multiple_of(s * 256 + c0, 128), 128)
                    phase_hi[r0 : r0 + MOM, at] = hi * sign
                    phase_lo[r0 : r0 + MOM, at] = lo * sign
            return carry

        lax.fori_loop(0, 8, phases, 0)
        momrow[...] = jnp.zeros_like(momrow)
        momrow[0:1, 0:n_mom] = mom[2:3]
        momrow[0:1, 64 : 64 + n_mom] = mom[2:3]
        loop_s[...] = jnp.zeros_like(loop_s)
        zero = jnp.zeros((4, 3, 8, 128), jnp.float32)
        field[5, 0] = zero
        field[5, 1] = zero

    def project(fr, fi, mu, sign):
        rows_r, rows_i = [], []
        for spin in range(2):
            col, power = UPPER[mu][spin]
            if sign < 0:
                power += 2
            r, i = add_times_i(power, (fr[spin], fi[spin]), (fr[2 + col], fi[2 + col]))
            rows_r.append(r)
            rows_i.append(i)
        return jnp.stack(rows_r), jnp.stack(rows_i)

    def add_up(acc, half, mu, sign):
        hr, hi = half
        for spin in range(2):
            acc[spin] = (hr[spin], hi[spin]) if acc[spin] is None else (acc[spin][0] + hr[spin], acc[spin][1] + hi[spin])
            col, power = LOWER[mu][spin]
            if sign < 0:
                power += 2
            term = (hr[col], hi[col])
            acc[2 + spin] = times_i(power, *term) if acc[2 + spin] is None else add_times_i(power, acc[2 + spin], term)

    def to_row(tiles):
        out = jnp.zeros((8, 128), jnp.float32)
        for k, tile in enumerate(tiles):
            for n in range(2):
                part = jnp.where(ev, tile, 0.0) if n == 0 else jnp.where(ev, 0.0, tile)
                out = jnp.where(row == 2 * k + n, jnp.sum(part, axis=0, keepdims=True), out)
        for by in (64, 32, 16):
            out = out + pltpu.roll(out, by, 1)
        return jnp.sum(jnp.where(lane >> 4 == row, out, 0.0), axis=0, keepdims=True)

    def from_row(line, k):
        return [
            jnp.sum(jnp.where(lane1 >> 4 == 2 * k + n, line, 0.0), axis=1, keepdims=True) for n in range(2)
        ]

    def row_send(group, slot, dst, stage):
        for k, offset in enumerate(group):
            pltpu.make_async_remote_copy(
                src_ref=row_s.at[slot, pl.ds(0, 1)], dst_ref=dst.at[pl.ds(k, 1)], send_sem=row_ssem.at[stage],
                recv_sem=row_rsem.at[stage], device_id=place(offset), device_id_type=MESH,
            ).start()

    def row_recv(slot, dst, stage):
        pltpu.make_async_copy(dst, dst, row_rsem.at[stage]).wait()
        return row_s[slot, 0:1, :] + jnp.sum(dst[...], axis=0, keepdims=True)

    first_r = (row_r0, row_r1, row_r2)

    def spread(pair):
        return jnp.where(ev, jnp.broadcast_to(pair[0], (8, 128)), jnp.broadcast_to(pair[1], (8, 128)))

    products = gamma_products()

    def project_loops(q, at_field, at_inner):
        for a in range(4):
            par_r, par_i = [], []
            for par, ref, at in ((0, field, at_field), (1, inner, at_inner)):
                br = bi = None
                for c in range(3):
                    sr, si = sfield[par, 0, a, c], sfield[par, 1, a, c]
                    pr, pi = ref[at, 0, :, c], ref[at, 1, :, c]
                    tr, ti = sr * pr + si * pi, sr * pi - si * pr
                    br, bi = (tr, ti) if br is None else (br + tr, bi + ti)
                par_r.append(br)
                par_i.append(bi)
            for re_im, (e, o) in enumerate((par_r, par_i)):
                bil[0, re_im, a] = jnp.where(ev, e, o)
                bil[1, re_im, a] = jnp.where(ev, o, e)

        def gammas(n, carry):
            for first in range(4):
                group = [g for g in range(16) if abs(products[g][0, first]) > 0.5]
                perm = [int(np.argmax(np.abs(products[group[0]][a]))) for a in range(4)]
                terms = [(bil[n, 0, a, perm[a]], bil[n, 1, a, perm[a]]) for a in range(4)]
                for g in group:
                    acc = None
                    for a in range(4):
                        power = int(round(np.angle(products[g][a, perm[a]]) / (math.pi / 2))) % 4
                        acc = times_i(power, *terms[a]) if acc is None else add_times_i(power, acc, terms[a])
                    for re_im in range(2):
                        start = pl.multiple_of((re_im * 32 + n * 16 + g) * 8, 8)
                        cur[pl.ds(start, 8), :] = acc[re_im]
            return carry

        lax.fori_loop(0, 2, gammas, 0)
        out = jnp.zeros((32, 128), jnp.float32)
        contract = (((1,), (1,)), ((), ()))
        for s in range(8):
            both = jnp.concatenate([cur[pl.ds(s, 32, stride=8), :], cur[pl.ds(256 + s, 32, stride=8), :]], axis=1)
            hi = both.astype(jnp.bfloat16)
            lo = (both - hi.astype(jnp.float32)).astype(jnp.bfloat16)
            wide = slice(s * 256, s * 256 + 256)
            ph, plo = phase_hi[:, wide], phase_lo[:, wide]
            main = lax.dot_general(jnp.concatenate([hi, lo], axis=0), ph, contract, preferred_element_type=jnp.float32)
            out = out + main[:32] + main[32:]
            out = out + lax.dot_general(hi, plo, contract, preferred_element_type=jnp.float32)
        loop_s[pl.ds(q, 32, stride=8), :] = out

    def loops_send():
        for k, offset in enumerate(ALONG_SPACE):
            target, _ = place(offset)
            pltpu.make_async_remote_copy(
                src_ref=loop_s.at[pl.ds(pl.multiple_of(target * 8, 8), 8)], dst_ref=loop_r.at[k],
                send_sem=loop_ssem, recv_sem=loop_rsem, device_id=(target, t), device_id_type=MESH,
            ).start()

    def main(core):
        far, near = (x_dn, x_up) if core == 0 else (x_up, x_dn)
        devices = ((far, t), (near, t), (x, t_dn), (x, t_up))
        sign_in = (1, -1, -1, 1) if core == 0 else (-1, 1, -1, 1)
        sign_out = (-1, 1, -1, 1) if core == 0 else (1, -1, -1, 1)
        axes = (0, 0, 3, 3)

        def copy(j, k):
            return pltpu.make_async_remote_copy(
                src_ref=send.at[j, k], dst_ref=recv.at[j, k], send_sem=send_sem, recv_sem=recv_sem.at[j, k],
                device_id=devices[k], device_id_type=MESH,
            )

        def post(j, k, par, fr, fi):
            half = project(fr, fi, axes[k], sign_out[k])
            if sign_out[k] > 0:
                half = color_apply(wlink.at[par, axes[k]], half, True)
            send[j, k, 0] = half[0]
            send[j, k, 1] = half[1]
            copy(j, k).start()

        def take(acc, j, k, to):
            copy(j, k).wait_recv()
            half = (recv[j, k, 0], recv[j, k, 1])
            if k == 0 and j > 0:
                half = (half[0] + echo[0], half[1] + echo[1])
            if sign_in[k] < 0:
                half = color_apply(wlink.at[to, axes[k]], half, False)
            add_up(acc, half, axes[k], sign_in[k])

        def stacked(acc):
            return jnp.stack([a[0] for a in acc]), jnp.stack([a[1] for a in acc])

        def message(j):
            if j == 0:
                return inner[4, 0], inner[4, 1]
            p = (j - 1) // 2
            if j % 2 == 0:
                return inner[p, 0], inner[p, 1]
            if p % 2 == 0:
                return flip(field[p, 0]), flip(field[p, 1])
            return field[p, 0], field[p, 1]

        def linear(j, fr, fi, clover):
            if j == 0:
                return KAPPA * fr, KAPPA * fi
            adjoint = (j - 1) // 2 % 2 == 0
            if j % 2 == 1:
                fr, fi = clover_apply(clover, fr, fi, adjoint)
                return KAPPA * fr, KAPPA * fi
            if adjoint:
                fr, fi = flip(fr), flip(fi)
            return -KAPPA * fr, -KAPPA * fi

        def outgoing(j, fr, fi):
            if j % 4 == 0:
                return flip(fr), flip(fi)
            return fr, fi

        def far_copy(k):
            src, dst = (far_send.at[k], far_recv.at[k]) if k < 2 else (link.at[0], far_raw)
            return pltpu.make_async_remote_copy(
                src_ref=src, dst_ref=dst, send_sem=far_ssem.at[k], recv_sem=far_rsem.at[k],
                device_id=devices[0], device_id_type=MESH,
            )

        def make_echo(j):
            par = j % 2
            if j == 1 and core == 0:
                far_copy(2).wait_recv()
                a = far_raw[...]
                b = move(a, 2, -1)
                far_link[0] = jnp.where(ev, b, a)
                far_link[1] = jnp.where(ev, a, b)
            if j == 2:
                for chi in range(2):
                    far_copy(chi).wait_recv()

                    def unpack(r, carry):
                        a = far_recv[chi, r]
                        far_clov[0, chi, r] = jnp.where(ev, a, move(a, 2, -1))
                        far_clov[1, chi, r] = jnp.where(ev, move(a, 2, 1), a)
                        return carry

                    lax.fori_loop(0, 6, unpack, 0)
            half = project(*message(j - 1), 0, sign_out[0])
            if core == 1:
                half = color_apply(wlink.at[par, 0], half, True)
            else:
                half = color_apply(far_link.at[1 - par], half, False)
            acc = [None] * 4
            add_up(acc, half, 0, sign_out[0])
            fr, fi = outgoing(j - 1, *linear(j - 1, *stacked(acc), far_clov))
            half = project(fr, fi, 0, sign_in[0])
            if core == 0:
                half = color_apply(far_link.at[1 - par], half, True)
            echo[0] = half[0]
            echo[1] = half[1]

        def early(j):
            if j == 0:
                if core == 1:
                    far_copy(2).start()
                for chi in range(2):

                    def pack(r, carry):
                        far_send[chi, r] = jnp.where(ev, wclov[1, 1, chi, r], wclov[1, 0, chi, r])
                        return carry

                    lax.fori_loop(0, 6, pack, 0)
                far_copy(0).start()
                pack_links((1, 2))
            if j == 1:
                far_copy(1).start()
            if j == 5:
                r0, r1 = field[1, 0], field[1, 1]
                i0, i1 = field[2, 0], field[2, 1]
                row_s[0, 0:1, :] = to_row([jnp.sum(a * a + b * b, axis=(0, 1)) for a, b in ((r0, r1), (i0, i1))])
                row_send(ROUNDS[0], 0, first_r[0], 0)
            if j in (6, 7):
                row_s[j - 5, 0:1, :] = row_recv(j - 6, first_r[j - 6], j - 6)
                row_send(ROUNDS[j - 5], j - 5, first_r[j - 5], j - 5)

        def late(j):
            if j == 0:
                pack_clover(0)
            if j == 1:
                make_phases()
            if j > 0 and j % 2 == 0:
                p = j // 2 - 1
                cr, ci = clover_apply(wclov.at[0], field[p, 0], field[p, 1], p % 2 == 0)
                base[0] = cr
                base[1] = ci
            if j == 4:
                project_loops(0, 5, 4)
            if j == 6:
                project_loops(1, 1, 1)
            if j == 8:
                line = row_recv(2, first_r[2], 2)
                row_s[3, 0:1, :] = line
                rr, image = from_row(line, 0), from_row(line, 1)
                alpha = spread([rr[n] / image[n] for n in range(2)])
                alpha_ref[0] = alpha
                alpha_odd = spread([rr[1 - n] / image[1 - n] for n in range(2)])
                sq = None
                for re_im in range(2):
                    r = field[1, re_im] - alpha * field[3, re_im]
                    field[6, re_im] = r
                    inner[5, re_im] = inner[1, re_im] - alpha_odd * inner[3, re_im]
                    part = jnp.sum(r * r, axis=(0, 1))
                    sq = part if sq is None else sq + part
                alpha_ref[1] = sq
                project_loops(2, 6, 5)
                loops_send()

        post(0, 0, 1, *message(0))
        for j in range(9):
            par, to = 1 - j % 2, j % 2
            p = (j - 1) // 2
            fr, fi = message(j)
            for k in (2, 3, 1):
                post(j, k, par, fr, fi)
            early(j)
            acc = [None] * 4
            for mu in (1, 2):
                hr, hi = project(fr, fi, mu, -1)
                ahead = (move(hr, mu, 1), move(hi, mu, 1))
                add_up(acc, color_apply(wlink.at[to, mu], ahead, False), mu, -1)
                hr, hi = color_apply(wlink.at[par, mu], project(fr, fi, mu, 1), True)
                add_up(acc, (move(hr, mu, -1), move(hi, mu, -1)), mu, 1)
            if j > 0:
                make_echo(j)
            late(j)
            for k in (1, 2, 3):
                take(acc, j, k, to)
            vr, vi = linear(j, *stacked(acc), wclov.at[1])
            if j % 2 == 0:
                start = (base[0], base[1]) if j > 0 else (sfield[0, 0], sfield[0, 1])
                vr, vi = start[0] + vr, start[1] + vi
            if j < 8:
                post(j + 1, 0, to, *outgoing(j, vr, vi))
            acc = [None] * 4
            take(acc, j, 0, to)
            lr, li = linear(j, *stacked(acc), wclov.at[1])
            store, at = (field, j // 2) if j % 2 == 0 else (inner, p)
            store[at, 0] = vr + lr
            store[at, 1] = vi + li
        for k in range(2 + core):
            far_copy(k).wait_send()

    loads[0].wait()
    for re_im in range(2):
        a = src[0, re_im]
        b = move(src[1, re_im], 2, -1)
        sfield[0, re_im] = jnp.where(ev, a, b)
        sfield[1, re_im] = jnp.where(ev, b, a)
    loads[1].wait()
    pack_links((0, 3))
    loads[2].wait()
    pack_clover(1)
    cr, ci = clover_apply(wclov.at[1], sfield[1, 0], sfield[1, 1], False)
    inner[4, 0] = cr
    inner[4, 1] = ci
    pl.semaphore_wait(barrier, len(greeted))
    for core in range(2):
        pl.when(x % 2 == core)(lambda core=core: main(core))

    alpha = alpha_ref[0]
    m1 = m2 = None
    for re_im in range(2):
        v, w = field[2, re_im] - alpha * field[4, re_im], field[2, re_im]
        a, b = jnp.sum(v * v, axis=(0, 1)), jnp.sum(v * w, axis=(0, 1))
        m1, m2 = (a, b) if m1 is None else (m1 + a, m2 + b)
    row_s[4, 0:1, :] = to_row([alpha_ref[1], m1, m2])
    row_send(EVERYONE, 4, last_r, 3)
    second = x >= n_space // 2
    angle = momrow[0:1, :].astype(jnp.int32) * second.astype(jnp.int32)
    cos, sin = cos_sin(angle & 31)
    sin = jnp.where(lane1 < 64, -sin, sin)
    pltpu.make_async_copy(loop_r, loop_r, loop_rsem).wait()
    own = loop_s[pl.ds(pl.multiple_of(x * 8, 8), 8), :]
    piece = own + jnp.sum(loop_r[...], axis=0)
    piece = piece * cos + pltpu.roll(piece, 64, 1) * sin
    piece = piece * (1.0 / math.sqrt(n_space * NY * NZ))
    start = row_s[3, 0:1, :]
    rr0, im0 = [jnp.where(second, v[1], v[0]) for v in (from_row(start, 0), from_row(start, 1))]
    line = row_recv(4, last_r, 3)
    rr1, m1, m2 = [jnp.where(second, v[1], v[0]) for v in (from_row(line, 0), from_row(line, 1), from_row(line, 2))]
    alpha0, beta = rr0 / im0, rr1 / rr0
    alpha1 = rr1 / (m1 + beta * (2.0 * m2 + beta * im0))
    line = piece[0:1] + (alpha0 + alpha1 * beta) * piece[1:2] + alpha1 * piece[2:3]
    out_ref[0] = line[:, 0:n_mom]
    out_ref[1] = line[:, 64 : 64 + n_mom]

    pltpu.make_async_copy(send, send, send_sem).wait()
    for stage, ref in enumerate((row_r0, row_r1, row_r2, last_r)):
        pltpu.make_async_copy(ref, ref, row_ssem.at[stage]).wait()
    pltpu.make_async_copy(loop_r, loop_r, loop_ssem).wait()


def solution(mesh):
    n_space, n_tm = mesh.shape["space"], mesh.shape["tm"]

    def local(sources, links, clover, momenta):
        f32 = jnp.float32
        n_mom = momenta.shape[0]
        tile = (8, 128)
        scratch = [
            pltpu.VMEM((2, 2, 4, 3) + tile, f32),
            pltpu.VMEM((2, 2, 6, 6) + tile, f32),
            pltpu.VMEM((4, 2, 3, 3) + tile, f32),
            pltpu.VMEM((3, n_mom), jnp.int32),
            pltpu.VMEM((2, 4, 2, 3, 3) + tile, f32),
            pltpu.VMEM((2, 2, 2, 6, 6) + tile, f32),
            pltpu.VMEM((2, 2, 4, 3) + tile, f32),
            pltpu.VMEM((7, 2, 4, 3) + tile, f32),
            pltpu.VMEM((6, 2, 4, 3) + tile, f32),
            pltpu.VMEM((2, 4, 3) + tile, f32),
            pltpu.VMEM((2, 2, 4, 4) + tile, f32),
            pltpu.VMEM((512, 128), f32),
            pltpu.VMEM((128, 2048), jnp.bfloat16),
            pltpu.VMEM((128, 2048), jnp.bfloat16),
            pltpu.VMEM(tile, f32),
            pltpu.VMEM((9, 4, 2, 2, 3) + tile, f32),
            pltpu.VMEM((9, 4, 2, 2, 3) + tile, f32),
            pltpu.VMEM((6,) + tile, f32),
            *[pltpu.VMEM((len(group), 128), f32) for group in ROUNDS + (EVERYONE,)],
            pltpu.VMEM((2,) + tile, f32),
            pltpu.VMEM((256, 128), f32),
            pltpu.VMEM((n_space - 1,) + tile, f32),
            pltpu.VMEM((2, 2, 6, 6) + tile, f32),
            pltpu.VMEM((2, 2, 3, 3) + tile, f32),
            pltpu.VMEM((2, 6, 6) + tile, f32),
            pltpu.VMEM((2, 6, 6) + tile, f32),
            pltpu.VMEM((2, 3, 3) + tile, f32),
            pltpu.VMEM((2, 2, 3) + tile, f32),
            pltpu.SemaphoreType.DMA((4,)),
            pltpu.SemaphoreType.DMA,
            pltpu.SemaphoreType.DMA((9, 4)),
            pltpu.SemaphoreType.DMA((5,)),
            pltpu.SemaphoreType.DMA((5,)),
            pltpu.SemaphoreType.DMA,
            pltpu.SemaphoreType.DMA,
            pltpu.SemaphoreType.DMA((3,)),
            pltpu.SemaphoreType.DMA((3,)),
        ]
        out = pl.pallas_call(
            lambda *refs: kernel(n_space, n_tm, *refs),
            out_shape=jax.ShapeDtypeStruct((2, 1, n_mom), f32),
            in_specs=[pl.BlockSpec(memory_space=pl.ANY)] * 4,
            out_specs=pl.BlockSpec(memory_space=pltpu.VMEM),
            scratch_shapes=scratch,
            compiler_params=pltpu.CompilerParams(
                collective_id=0, has_side_effects=True, vmem_limit_bytes=48 * 1024 * 1024
            ),
            name="loops",
        )(
            *[
                pltpu.with_memory_space_constraint(v, pltpu.HBM)
                for v in (
                    sources.reshape((2, 2, 4, 3) + tile),
                    clover.reshape((2, 2, 6, 6) + tile),
                    links.reshape((4, 2, 3, 3) + tile),
                    momenta.T,
                )
            ]
        )
        return out.reshape(2, 1, n_mom, 1)

    placed = P(None, None, None, None, "space", "tm", None)
    return jax.shard_map(
        local, mesh=mesh, in_specs=(placed, placed, placed, P()), out_specs=P(None, "space", None, "tm"), check_vma=False
    )
```

```python
import math

import jax
import jax.numpy as jnp
import numpy as np
from jax import lax
from jax.experimental import pallas as pl
from jax.experimental.pallas import tpu as pltpu
from jax.sharding import PartitionSpec as P

MESH = pl.DeviceIdType.MESH
NZ = 32
NY = 32
KAPPA = 0.1
HALVES = (slice(0, 4), slice(4, 8))
PARTS = (HALVES, (slice(0, 8),), HALVES, HALVES)
MOM = 48


UPPER = (((1, 1), (0, 1)), ((1, 0), (0, 2)), ((0, 1), (1, 3)), ((0, 0), (1, 0)))
LOWER = (((1, 3), (0, 3)), ((1, 2), (0, 0)), ((0, 3), (1, 1)), ((0, 0), (1, 0)))


def gamma_products():
    sigma = [
        np.array([[0, 1], [1, 0]]) + 0j,
        np.array([[0, -1j], [1j, 0]]),
        np.array([[1, 0], [0, -1]]) + 0j,
    ]
    zero = np.zeros((2, 2)) + 0j
    singles = [np.block([[zero, 1j * s], [-1j * s, zero]]) for s in sigma]
    singles.append(np.block([[zero, np.eye(2)], [np.eye(2), zero]]) + 0j)
    products = []
    for bits in range(16):
        product = np.eye(4) + 0j
        for direction in range(4):
            if bits >> direction & 1:
                product = product @ singles[direction]
        products.append(product)
    return products


def times_i(power, re, im):
    power %= 4
    if power == 0:
        return re, im
    if power == 1:
        return -im, re
    if power == 2:
        return -re, -im
    return im, -re


def add_times_i(power, acc, term):
    (ar, ai), (re, im) = acc, term
    power %= 4
    if power == 0:
        return ar + re, ai + im
    if power == 1:
        return ar - im, ai + re
    if power == 2:
        return ar - re, ai - im
    return ar + im, ai - re


def color_apply(link, half, adjoint):
    hr, hi = half
    outr = outi = None
    for b in range(3):
        if adjoint:
            ur, ui = link[0, b], link[1, b]
        else:
            ur, ui = link[0, :, b], link[1, :, b]
        ur, ui = ur[None], ui[None]
        xr, xi = hr[:, b][:, None], hi[:, b][:, None]
        if adjoint:
            tr, ti = ur * xr + ui * xi, ur * xi - ui * xr
        else:
            tr, ti = ur * xr - ui * xi, ur * xi + ui * xr
        outr, outi = (tr, ti) if outr is None else (outr + tr, outi + ti)
    return outr, outi


def clover_apply(mat, fr, fi, adjoint):
    tile = fr.shape[2:]
    xr, xi = fr.reshape((2, 6) + tile), fi.reshape((2, 6) + tile)
    outr = outi = None
    for i in range(6):
        vr, vi = xr[:, i][:, None], xi[:, i][:, None]
        if adjoint:
            cr, ci = mat[0, :, i], mat[1, :, i]
            tr, ti = cr * vr + ci * vi, cr * vi - ci * vr
        else:
            cr, ci = mat[0, :, :, i], mat[1, :, :, i]
            tr, ti = cr * vr - ci * vi, cr * vi + ci * vr
        outr, outi = (tr, ti) if outr is None else (outr + tr, outi + ti)
    return outr.reshape((4, 3) + tile), outi.reshape((4, 3) + tile)


def flip(v):
    return jnp.concatenate([v[:2], -v[2:]], axis=0)


def fan(ys, xs, cores, zs):
    offsets = [(y, x, c, z) for y in ys for x in xs for c in cores for z in zs if (y, x, c, z) != (0, 0, 0, 0)]
    return sorted(offsets, key=lambda o: -(min(o[0], 4 - o[0]) + min(o[1], 4 - o[1]) + min(o[3], 4 - o[3])))


ALONG_ROW = fan([0], range(4), range(2), [0])
ALONG_Y = fan(range(4), [0], [0], [0])
ALONG_Z = fan([0], [0], [0], range(4))
ALONG_SPACE = fan(range(4), range(4), range(2), [0])
EVERYONE = fan(range(4), range(4), range(2), range(4))
ROUNDS = (ALONG_ROW, ALONG_Y, ALONG_Z)


def kernel(
    n_space, n_tm,
    src_hbm, clov_hbm, link_hbm, mom_hbm, out_ref,
    src, clov, link, mom_ref, wlink, wclov, sfield, field, inner, base, bil, cur, phase_hi, phase_lo, momrow,
    send, recv, row_s, row_r0, row_r1, row_r2, last_r, alpha_ref, loop_s, loop_r, far_clov, far_link, far_send, far_recv, far_raw, echo, partial,
    in_sem, send_sem, recv_sem, row_ssem, row_rsem, loop_ssem, loop_rsem, far_ssem, far_rsem,
):
    x = lax.axis_index("space")
    t = lax.axis_index("tm")
    x_up, x_dn = lax.rem(x + 1, n_space), lax.rem(x + n_space - 1, n_space)
    t_up, t_dn = lax.rem(t + 1, n_tm), lax.rem(t + n_tm - 1, n_tm)

    loads = [
        pltpu.make_async_copy(a, b, in_sem.at[k])
        for k, (a, b) in enumerate(((src_hbm, src), (link_hbm, link), (clov_hbm, clov), (mom_hbm, mom_ref)))
    ]
    for load in loads:
        load.start()

    def space_at(dy, dx, dc):
        return ((x // 8 + dy) & 3) * 8 + (((x // 2) + dx) & 3) * 2 + ((x + dc) & 1)

    def place(offset):
        dy, dx, dc, dz = offset
        return (space_at(dy, dx, dc), (t + dz) & 3)

    barrier = pltpu.get_barrier_semaphore()
    greeted = [(x_up, t), (x_dn, t)] + [place(offset) for group in ROUNDS for offset in group]
    for device in greeted:
        pl.semaphore_signal(barrier, inc=1, device_id=device, device_id_type=MESH)

    lane = lax.broadcasted_iota(jnp.int32, (8, 128), 1)
    row = lax.broadcasted_iota(jnp.int32, (8, 128), 0)
    lane1 = lax.broadcasted_iota(jnp.int32, (1, 128), 1)
    zc = lane & 31
    yc = row * 4 + (lane >> 5)
    ev = ((yc + zc + x + t) & 1) == 0

    def move(v, axis, by):
        last = v.ndim - 1
        if axis == 2:
            if by == 1:
                return jnp.where(zc == 31, pltpu.roll(v, 31, last), pltpu.roll(v, 127, last))
            return jnp.where(zc == 0, pltpu.roll(v, 97, last), pltpu.roll(v, 1, last))
        if by == 1:
            a = pltpu.roll(v, 96, last)
            return jnp.where(lane >= 96, pltpu.roll(a, 7, last - 1), a)
        a = pltpu.roll(v, 32, last)
        return jnp.where(lane < 32, pltpu.roll(a, 1, last - 1), a)

    def cos_sin(k):
        a = (k - 16).astype(jnp.float32) * (math.pi / 32)
        q = a * a
        s = 1.0 / math.factorial(11)
        for m in (9, 7, 5, 3, 1):
            s = 1.0 / math.factorial(m) - q * s
        s = s * a
        c = 1.0 / math.factorial(12)
        for m in (10, 8, 6, 4, 2, 0):
            c = 1.0 / math.factorial(m) - q * c
        return 2.0 * s * s - 1.0, -2.0 * s * c

    def pack_clover(par):
        def step(k, carry):
            re_im, chi, r = k // 12, (k // 6) % 2, k % 6
            a = clov[re_im, chi, r]
            b = move(a, 2, -1)
            wclov[par, re_im, chi, r] = jnp.where(ev, a, b) if par == 0 else jnp.where(ev, b, a)
            return carry

        lax.fori_loop(0, 24, step, 0)

    t_sign = jnp.where(t == n_tm - 1, -1.0, 1.0).astype(jnp.float32)

    def pack_links(directions):
        for mu in directions:
            for re_im in range(2):
                a = link[mu, re_im]
                if mu == 3:
                    a = a * t_sign
                b = move(a, 2, -1)
                wlink[0, mu, re_im] = jnp.where(ev, a, b)
                wlink[1, mu, re_im] = jnp.where(ev, b, a)

    n_mom = mom_ref.shape[1]

    def make_phases():
        loads[3].wait()
        mom = mom_ref[...].astype(jnp.float32)
        eye = lax.broadcasted_iota(jnp.int32, (MOM, n_mom), 0) == lax.broadcasted_iota(jnp.int32, (MOM, n_mom), 1)
        columns = [
            jnp.sum(jnp.where(eye, jnp.broadcast_to(mom[k : k + 1], (MOM, n_mom)), 0.0), axis=1, keepdims=True).astype(jnp.int32)
            for k in range(3)
        ]
        zero_rows = jnp.zeros((64 - MOM, 2048), jnp.bfloat16)
        for ref in (phase_hi, phase_lo):
            ref[MOM:64, :] = zero_rows
            ref[64 + MOM : 128, :] = zero_rows

        def phases(s, carry):
            yrow = s * 4 + (lane1 >> 5)
            zrow = lane1 & 31
            c, sn = cos_sin((columns[0] * x + columns[1] * yrow + columns[2] * zrow) & 31)
            for value, places in ((c, ((0, 0, 1), (64, 128, 1))), (sn, ((0, 128, 1), (64, 0, -1)))):
                hi = value.astype(jnp.bfloat16)
                lo = (value - hi.astype(jnp.float32)).astype(jnp.bfloat16)
                for r0, c0, sign in places:
                    at = pl.ds(pl.multiple_of(s * 256 + c0, 128), 128)
                    phase_hi[r0 : r0 + MOM, at] = hi * sign
                    phase_lo[r0 : r0 + MOM, at] = lo * sign
            return carry

        lax.fori_loop(0, 8, phases, 0)
        momrow[...] = jnp.zeros_like(momrow)
        momrow[0:1, 0:n_mom] = mom[2:3]
        momrow[0:1, 64 : 64 + n_mom] = mom[2:3]
        loop_s[...] = jnp.zeros_like(loop_s)
        zero = jnp.zeros((4, 3, 8, 128), jnp.float32)
        field[5, 0] = zero
        field[5, 1] = zero

    def project(fr, fi, mu, sign):
        rows_r, rows_i = [], []
        for spin in range(2):
            col, power = UPPER[mu][spin]
            if sign < 0:
                power += 2
            r, i = add_times_i(power, (fr[spin], fi[spin]), (fr[2 + col], fi[2 + col]))
            rows_r.append(r)
            rows_i.append(i)
        return jnp.stack(rows_r), jnp.stack(rows_i)

    def add_up(acc, half, mu, sign):
        hr, hi = half
        for spin in range(2):
            acc[spin] = (hr[spin], hi[spin]) if acc[spin] is None else (acc[spin][0] + hr[spin], acc[spin][1] + hi[spin])
            col, power = LOWER[mu][spin]
            if sign < 0:
                power += 2
            term = (hr[col], hi[col])
            acc[2 + spin] = times_i(power, *term) if acc[2 + spin] is None else add_times_i(power, acc[2 + spin], term)

    def to_row(tiles):
        out = jnp.zeros((8, 128), jnp.float32)
        for k, tile in enumerate(tiles):
            for n in range(2):
                part = jnp.where(ev, tile, 0.0) if n == 0 else jnp.where(ev, 0.0, tile)
                out = jnp.where(row == 2 * k + n, jnp.sum(part, axis=0, keepdims=True), out)
        for by in (64, 32, 16):
            out = out + pltpu.roll(out, by, 1)
        return jnp.sum(jnp.where(lane >> 4 == row, out, 0.0), axis=0, keepdims=True)

    def from_row(line, k):
        return [
            jnp.sum(jnp.where(lane1 >> 4 == 2 * k + n, line, 0.0), axis=1, keepdims=True) for n in range(2)
        ]

    def row_send(group, slot, dst, stage):
        for k, offset in enumerate(group):
            pltpu.make_async_remote_copy(
                src_ref=row_s.at[slot, pl.ds(0, 1)], dst_ref=dst.at[pl.ds(k, 1)], send_sem=row_ssem.at[stage],
                recv_sem=row_rsem.at[stage], device_id=place(offset), device_id_type=MESH,
            ).start()

    def row_recv(slot, dst, stage):
        pltpu.make_async_copy(dst, dst, row_rsem.at[stage]).wait()
        return row_s[slot, 0:1, :] + jnp.sum(dst[...], axis=0, keepdims=True)

    first_r = (row_r0, row_r1, row_r2)

    def spread(pair):
        return jnp.where(ev, jnp.broadcast_to(pair[0], (8, 128)), jnp.broadcast_to(pair[1], (8, 128)))

    products = gamma_products()

    def project_loops(q, at_field, at_inner):
        for a in range(4):
            par_r, par_i = [], []
            for par, ref, at in ((0, field, at_field), (1, inner, at_inner)):
                br = bi = None
                for c in range(3):
                    sr, si = sfield[par, 0, a, c], sfield[par, 1, a, c]
                    pr, pi = ref[at, 0, :, c], ref[at, 1, :, c]
                    tr, ti = sr * pr + si * pi, sr * pi - si * pr
                    br, bi = (tr, ti) if br is None else (br + tr, bi + ti)
                par_r.append(br)
                par_i.append(bi)
            for re_im, (e, o) in enumerate((par_r, par_i)):
                bil[0, re_im, a] = jnp.where(ev, e, o)
                bil[1, re_im, a] = jnp.where(ev, o, e)

        def gammas(n, carry):
            for first in range(4):
                group = [g for g in range(16) if abs(products[g][0, first]) > 0.5]
                perm = [int(np.argmax(np.abs(products[group[0]][a]))) for a in range(4)]
                terms = [(bil[n, 0, a, perm[a]], bil[n, 1, a, perm[a]]) for a in range(4)]
                for g in group:
                    acc = None
                    for a in range(4):
                        power = int(round(np.angle(products[g][a, perm[a]]) / (math.pi / 2))) % 4
                        acc = times_i(power, *terms[a]) if acc is None else add_times_i(power, acc, terms[a])
                    for re_im in range(2):
                        start = pl.multiple_of((re_im * 32 + n * 16 + g) * 8, 8)
                        cur[pl.ds(start, 8), :] = acc[re_im]
            return carry

        lax.fori_loop(0, 2, gammas, 0)
        out = jnp.zeros((32, 128), jnp.float32)
        contract = (((1,), (1,)), ((), ()))
        for s in range(8):
            both = jnp.concatenate([cur[pl.ds(s, 32, stride=8), :], cur[pl.ds(256 + s, 32, stride=8), :]], axis=1)
            hi = both.astype(jnp.bfloat16)
            lo = (both - hi.astype(jnp.float32)).astype(jnp.bfloat16)
            wide = slice(s * 256, s * 256 + 256)
            ph, plo = phase_hi[:, wide], phase_lo[:, wide]
            main = lax.dot_general(jnp.concatenate([hi, lo], axis=0), ph, contract, preferred_element_type=jnp.float32)
            out = out + main[:32] + main[32:]
            out = out + lax.dot_general(hi, plo, contract, preferred_element_type=jnp.float32)
        loop_s[pl.ds(q, 32, stride=8), :] = out

    def loops_send():
        for k, offset in enumerate(ALONG_SPACE):
            target, _ = place(offset)
            pltpu.make_async_remote_copy(
                src_ref=loop_s.at[pl.ds(pl.multiple_of(target * 8, 8), 3)], dst_ref=loop_r.at[k, pl.ds(0, 3)],
                send_sem=loop_ssem, recv_sem=loop_rsem, device_id=(target, t), device_id_type=MESH,
            ).start()

    def main(core):
        far, near = (x_dn, x_up) if core == 0 else (x_up, x_dn)
        devices = ((far, t), (near, t), (x, t_dn), (x, t_up))
        sign_in = (1, -1, -1, 1) if core == 0 else (-1, 1, -1, 1)
        sign_out = (-1, 1, -1, 1) if core == 0 else (1, -1, -1, 1)
        axes = (0, 0, 3, 3)

        def copy(j, k, part):
            at = PARTS[k][part]
            return pltpu.make_async_remote_copy(
                src_ref=send.at[j, k, :, :, :, at], dst_ref=recv.at[j, k, :, :, :, at], send_sem=send_sem,
                recv_sem=recv_sem.at[j, k, part], device_id=devices[k], device_id_type=MESH,
            )

        def post(j, k, part, par, fr, fi):
            at = PARTS[k][part]
            half = project(fr, fi, axes[k], sign_out[k])
            if sign_out[k] > 0:
                half = color_apply(wlink.at[par, axes[k], :, :, :, at], half, True)
            send[j, k, 0, :, :, at] = half[0]
            send[j, k, 1, :, :, at] = half[1]
            copy(j, k, part).start()

        def take(acc, j, k, part, to):
            at = PARTS[k][part]
            copy(j, k, part).wait_recv()
            half = (recv[j, k, 0, :, :, at], recv[j, k, 1, :, :, at])
            if k == 0 and j > 0:
                half = (half[0] + echo[0, :, :, at], half[1] + echo[1, :, :, at])
            if sign_in[k] < 0:
                half = color_apply(wlink.at[to, axes[k], :, :, :, at], half, False)
            add_up(acc, half, axes[k], sign_in[k])

        def stacked(acc):
            return jnp.stack([a[0] for a in acc]), jnp.stack([a[1] for a in acc])

        def message(j, at=slice(0, 8)):
            if j == 0:
                return inner[4, 0, :, :, at], inner[4, 1, :, :, at]
            p = (j - 1) // 2
            if j % 2 == 0:
                return inner[p, 0, :, :, at], inner[p, 1, :, :, at]
            fr, fi = field[p, 0, :, :, at], field[p, 1, :, :, at]
            return (flip(fr), flip(fi)) if p % 2 == 0 else (fr, fi)

        def linear(j, fr, fi, clover):
            if j == 0:
                return KAPPA * fr, KAPPA * fi
            adjoint = (j - 1) // 2 % 2 == 0
            if j % 2 == 1:
                fr, fi = clover_apply(clover, fr, fi, adjoint)
                return KAPPA * fr, KAPPA * fi
            if adjoint:
                fr, fi = flip(fr), flip(fi)
            return -KAPPA * fr, -KAPPA * fi

        def outgoing(j, fr, fi):
            if j % 4 == 0:
                return flip(fr), flip(fi)
            return fr, fi

        def far_copy(k):
            src, dst = (far_send.at[k], far_recv.at[k]) if k < 2 else (link.at[0], far_raw)
            return pltpu.make_async_remote_copy(
                src_ref=src, dst_ref=dst, send_sem=far_ssem.at[k], recv_sem=far_rsem.at[k],
                device_id=devices[0], device_id_type=MESH,
            )

        def make_echo(j):
            par = j % 2
            if j == 1 and core == 0:
                far_copy(2).wait_recv()
                a = far_raw[...]
                b = move(a, 2, -1)
                far_link[0] = jnp.where(ev, b, a)
                far_link[1] = jnp.where(ev, a, b)
            if j == 2:
                for chi in range(2):
                    far_copy(chi).wait_recv()

                    def unpack(r, carry):
                        a = far_recv[chi, r]
                        far_clov[0, chi, r] = jnp.where(ev, a, move(a, 2, -1))
                        far_clov[1, chi, r] = jnp.where(ev, move(a, 2, 1), a)
                        return carry

                    lax.fori_loop(0, 6, unpack, 0)
            half = project(*message(j - 1), 0, sign_out[0])
            if core == 1:
                half = color_apply(wlink.at[par, 0], half, True)
            else:
                half = color_apply(far_link.at[1 - par], half, False)
            acc = [None] * 4
            add_up(acc, half, 0, sign_out[0])
            fr, fi = outgoing(j - 1, *linear(j - 1, *stacked(acc), far_clov))
            half = project(fr, fi, 0, sign_in[0])
            if core == 0:
                half = color_apply(far_link.at[1 - par], half, True)
            echo[0] = half[0]
            echo[1] = half[1]

        def early(j):
            if j == 0:
                if core == 1:
                    far_copy(2).start()
                pack_clover(1)
                for chi in range(2):

                    def pack(r, carry):
                        far_send[chi, r] = jnp.where(ev, wclov[1, 1, chi, r], wclov[1, 0, chi, r])
                        return carry

                    lax.fori_loop(0, 6, pack, 0)
                far_copy(0).start()
                pack_links((1, 2))
            if j == 1:
                far_copy(1).start()
            if j == 5:
                r0, r1 = field[1, 0], field[1, 1]
                i0, i1 = field[2, 0], field[2, 1]
                row_s[0, 0:1, :] = to_row([jnp.sum(a * a + b * b, axis=(0, 1)) for a, b in ((r0, r1), (i0, i1))])
                row_send(ROUNDS[0], 0, first_r[0], 0)
            if j in (6, 7):
                row_s[j - 5, 0:1, :] = row_recv(j - 6, first_r[j - 6], j - 6)
                row_send(ROUNDS[j - 5], j - 5, first_r[j - 5], j - 5)

        def late(j):
            if j == 0:
                pack_clover(0)
            if j == 1:
                make_phases()
            if j > 0 and j % 2 == 0:
                p = j // 2 - 1
                cr, ci = clover_apply(wclov.at[0], field[p, 0], field[p, 1], p % 2 == 0)
                base[0] = cr
                base[1] = ci
            if j == 4:
                project_loops(0, 5, 4)
            if j == 6:
                project_loops(1, 1, 1)
            if j == 8:
                line = row_recv(2, first_r[2], 2)
                row_s[3, 0:1, :] = line
                rr, image = from_row(line, 0), from_row(line, 1)
                alpha = spread([rr[n] / image[n] for n in range(2)])
                alpha_ref[0] = alpha
                alpha_odd = spread([rr[1 - n] / image[1 - n] for n in range(2)])
                sq = None
                for re_im in range(2):
                    r = field[1, re_im] - alpha * field[3, re_im]
                    field[6, re_im] = r
                    inner[5, re_im] = inner[1, re_im] - alpha_odd * inner[3, re_im]
                    part = jnp.sum(r * r, axis=(0, 1))
                    sq = part if sq is None else sq + part
                alpha_ref[1] = sq
                project_loops(2, 6, 5)
                loops_send()

        for part in range(2):
            post(0, 0, part, 1, *message(0, HALVES[part]))
        for part in range(2):
            for k in (2, 3):
                post(0, k, part, 1, *message(0, HALVES[part]))
        for j in range(9):
            par, to = 1 - j % 2, j % 2
            p = (j - 1) // 2
            fr, fi = message(j)
            post(j, 1, 0, par, fr, fi)
            early(j)
            acc = [None] * 4
            for mu in (1, 2):
                hr, hi = project(fr, fi, mu, -1)
                ahead = (move(hr, mu, 1), move(hi, mu, 1))
                add_up(acc, color_apply(wlink.at[to, mu], ahead, False), mu, -1)
                hr, hi = color_apply(wlink.at[par, mu], project(fr, fi, mu, 1), True)
                add_up(acc, (move(hr, mu, -1), move(hi, mu, -1)), mu, 1)
            if j > 0:
                make_echo(j)
            late(j)
            take(acc, j, 1, 0, to)
            partial[0], partial[1] = stacked(acc)
            for part, at in enumerate(HALVES):
                acc = [(partial[0, spin, :, at], partial[1, spin, :, at]) for spin in range(4)]
                for k in (2, 3):
                    take(acc, j, k, part, to)
                vr, vi = linear(j, *stacked(acc), wclov.at[1, :, :, :, :, at])
                if j % 2 == 0:
                    start, first = (base, ()) if j > 0 else (sfield, (0,))
                    vr = start[first + (0, slice(None), slice(None), at)] + vr
                    vi = start[first + (1, slice(None), slice(None), at)] + vi
                partial[0, :, :, at] = vr
                partial[1, :, :, at] = vi
                if j < 8:
                    post(j + 1, 0, part, to, *outgoing(j, vr, vi))
            for part, at in enumerate(HALVES):
                acc = [None] * 4
                take(acc, j, 0, part, to)
                lr, li = linear(j, *stacked(acc), wclov.at[1, :, :, :, :, at])
                vr, vi = partial[0, :, :, at] + lr, partial[1, :, :, at] + li
                store, slot = (field, j // 2) if j % 2 == 0 else (inner, p)
                store[slot, 0, :, :, at] = vr
                store[slot, 1, :, :, at] = vi
                if j < 8:
                    for k in (2, 3):
                        post(j + 1, k, part, to, *outgoing(j, vr, vi))
        for k in range(2 + core):
            far_copy(k).wait_send()

    loads[0].wait()
    for re_im in range(2):
        a = src[0, re_im]
        b = move(src[1, re_im], 2, -1)
        sfield[0, re_im] = jnp.where(ev, a, b)
        sfield[1, re_im] = jnp.where(ev, b, a)
    loads[1].wait()
    pack_links((0, 3))
    loads[2].wait()
    both = [clover_apply(clov, src[n, 0], src[n, 1], False) for n in range(2)]
    for re_im in range(2):
        inner[4, re_im] = jnp.where(ev, move(both[1][re_im], 2, -1), both[0][re_im])
    pl.semaphore_wait(barrier, len(greeted))
    for core in range(2):
        pl.when(x % 2 == core)(lambda core=core: main(core))

    alpha = alpha_ref[0]
    m1 = m2 = None
    for re_im in range(2):
        v, w = field[2, re_im] - alpha * field[4, re_im], field[2, re_im]
        a, b = jnp.sum(v * v, axis=(0, 1)), jnp.sum(v * w, axis=(0, 1))
        m1, m2 = (a, b) if m1 is None else (m1 + a, m2 + b)
    row_s[4, 0:1, :] = to_row([alpha_ref[1], m1, m2])
    row_send(EVERYONE, 4, last_r, 3)
    second = x >= n_space // 2
    angle = momrow[0:1, :].astype(jnp.int32) * second.astype(jnp.int32)
    cos, sin = cos_sin(angle & 31)
    sin = jnp.where(lane1 < 64, -sin, sin)
    pieces = loop_r.at[:, pl.ds(0, 3)]
    pltpu.make_async_copy(pieces, pieces, loop_rsem).wait()
    own = loop_s[pl.ds(pl.multiple_of(x * 8, 8), 3), :]
    piece = own + jnp.sum(loop_r[:, 0:3, :], axis=0)
    piece = piece * cos + pltpu.roll(piece, 64, 1) * sin
    piece = piece * (1.0 / math.sqrt(n_space * NY * NZ))
    start = row_s[3, 0:1, :]
    rr0, im0 = [jnp.where(second, v[1], v[0]) for v in (from_row(start, 0), from_row(start, 1))]
    line = row_recv(4, last_r, 3)
    rr1, m1, m2 = [jnp.where(second, v[1], v[0]) for v in (from_row(line, 0), from_row(line, 1), from_row(line, 2))]
    alpha0, beta = rr0 / im0, rr1 / rr0
    alpha1 = rr1 / (m1 + beta * (2.0 * m2 + beta * im0))
    line = piece[0:1] + (alpha0 + alpha1 * beta) * piece[1:2] + alpha1 * piece[2:3]
    out_ref[0] = line[:, 0:n_mom]
    out_ref[1] = line[:, 64 : 64 + n_mom]

    pltpu.make_async_copy(send, send, send_sem).wait()
    for stage, ref in enumerate((row_r0, row_r1, row_r2, last_r)):
        pltpu.make_async_copy(ref, ref, row_ssem.at[stage]).wait()
    pltpu.make_async_copy(pieces, pieces, loop_ssem).wait()


def solution(mesh):
    n_space, n_tm = mesh.shape["space"], mesh.shape["tm"]

    def local(sources, links, clover, momenta):
        f32 = jnp.float32
        n_mom = momenta.shape[0]
        tile = (8, 128)
        scratch = [
            pltpu.VMEM((2, 2, 4, 3) + tile, f32),
            pltpu.VMEM((2, 2, 6, 6) + tile, f32),
            pltpu.VMEM((4, 2, 3, 3) + tile, f32),
            pltpu.VMEM((3, n_mom), jnp.int32),
            pltpu.VMEM((2, 4, 2, 3, 3) + tile, f32),
            pltpu.VMEM((2, 2, 2, 6, 6) + tile, f32),
            pltpu.VMEM((2, 2, 4, 3) + tile, f32),
            pltpu.VMEM((7, 2, 4, 3) + tile, f32),
            pltpu.VMEM((6, 2, 4, 3) + tile, f32),
            pltpu.VMEM((2, 4, 3) + tile, f32),
            pltpu.VMEM((2, 2, 4, 4) + tile, f32),
            pltpu.VMEM((512, 128), f32),
            pltpu.VMEM((128, 2048), jnp.bfloat16),
            pltpu.VMEM((128, 2048), jnp.bfloat16),
            pltpu.VMEM(tile, f32),
            pltpu.VMEM((9, 4, 2, 2, 3) + tile, f32),
            pltpu.VMEM((9, 4, 2, 2, 3) + tile, f32),
            pltpu.VMEM((6,) + tile, f32),
            *[pltpu.VMEM((len(group), 128), f32) for group in ROUNDS + (EVERYONE,)],
            pltpu.VMEM((2,) + tile, f32),
            pltpu.VMEM((256, 128), f32),
            pltpu.VMEM((n_space - 1,) + tile, f32),
            pltpu.VMEM((2, 2, 6, 6) + tile, f32),
            pltpu.VMEM((2, 2, 3, 3) + tile, f32),
            pltpu.VMEM((2, 6, 6) + tile, f32),
            pltpu.VMEM((2, 6, 6) + tile, f32),
            pltpu.VMEM((2, 3, 3) + tile, f32),
            pltpu.VMEM((2, 2, 3) + tile, f32),
            pltpu.VMEM((2, 4, 3) + tile, f32),
            pltpu.SemaphoreType.DMA((4,)),
            pltpu.SemaphoreType.DMA,
            pltpu.SemaphoreType.DMA((9, 4, 2)),
            pltpu.SemaphoreType.DMA((5,)),
            pltpu.SemaphoreType.DMA((5,)),
            pltpu.SemaphoreType.DMA,
            pltpu.SemaphoreType.DMA,
            pltpu.SemaphoreType.DMA((3,)),
            pltpu.SemaphoreType.DMA((3,)),
        ]
        out = pl.pallas_call(
            lambda *refs: kernel(n_space, n_tm, *refs),
            out_shape=jax.ShapeDtypeStruct((2, 1, n_mom), f32),
            in_specs=[pl.BlockSpec(memory_space=pl.ANY)] * 4,
            out_specs=pl.BlockSpec(memory_space=pltpu.VMEM),
            scratch_shapes=scratch,
            compiler_params=pltpu.CompilerParams(
                collective_id=0, has_side_effects=True, vmem_limit_bytes=48 * 1024 * 1024
            ),
            name="loops",
        )(
            *[
                pltpu.with_memory_space_constraint(v, pltpu.HBM)
                for v in (
                    sources.reshape((2, 2, 4, 3) + tile),
                    clover.reshape((2, 2, 6, 6) + tile),
                    links.reshape((4, 2, 3, 3) + tile),
                    momenta.T,
                )
            ]
        )
        return out.reshape(2, 1, n_mom, 1)

    placed = P(None, None, None, None, "space", "tm", None)
    return jax.shard_map(
        local, mesh=mesh, in_specs=(placed, placed, placed, P()), out_specs=P(None, "space", None, "tm"), check_vma=False
    )
```

```python
import math

import jax
import jax.numpy as jnp
import numpy as np
from jax import lax
from jax.experimental import pallas as pl
from jax.experimental.pallas import tpu as pltpu
from jax.sharding import PartitionSpec as P

MESH = pl.DeviceIdType.MESH
NZ = 32
NY = 32
KAPPA = 0.1
HALVES = (slice(0, 4), slice(4, 8))
PARTS = (HALVES, (slice(0, 8),), HALVES, HALVES)
MOM = 48


UPPER = (((1, 1), (0, 1)), ((1, 0), (0, 2)), ((0, 1), (1, 3)), ((0, 0), (1, 0)))
LOWER = (((1, 3), (0, 3)), ((1, 2), (0, 0)), ((0, 3), (1, 1)), ((0, 0), (1, 0)))


def gamma_products():
    sigma = [
        np.array([[0, 1], [1, 0]]) + 0j,
        np.array([[0, -1j], [1j, 0]]),
        np.array([[1, 0], [0, -1]]) + 0j,
    ]
    zero = np.zeros((2, 2)) + 0j
    singles = [np.block([[zero, 1j * s], [-1j * s, zero]]) for s in sigma]
    singles.append(np.block([[zero, np.eye(2)], [np.eye(2), zero]]) + 0j)
    products = []
    for bits in range(16):
        product = np.eye(4) + 0j
        for direction in range(4):
            if bits >> direction & 1:
                product = product @ singles[direction]
        products.append(product)
    return products


def times_i(power, re, im):
    power %= 4
    if power == 0:
        return re, im
    if power == 1:
        return -im, re
    if power == 2:
        return -re, -im
    return im, -re


def add_times_i(power, acc, term):
    (ar, ai), (re, im) = acc, term
    power %= 4
    if power == 0:
        return ar + re, ai + im
    if power == 1:
        return ar - im, ai + re
    if power == 2:
        return ar - re, ai - im
    return ar + im, ai - re


def color_apply(link, half, adjoint):
    hr, hi = half
    outr = outi = None
    for b in range(3):
        if adjoint:
            ur, ui = link[0, b], link[1, b]
        else:
            ur, ui = link[0, :, b], link[1, :, b]
        ur, ui = ur[None], ui[None]
        xr, xi = hr[:, b][:, None], hi[:, b][:, None]
        if adjoint:
            tr, ti = ur * xr + ui * xi, ur * xi - ui * xr
        else:
            tr, ti = ur * xr - ui * xi, ur * xi + ui * xr
        outr, outi = (tr, ti) if outr is None else (outr + tr, outi + ti)
    return outr, outi


def clover_apply(mat, fr, fi, adjoint):
    tile = fr.shape[2:]
    xr, xi = fr.reshape((2, 6) + tile), fi.reshape((2, 6) + tile)
    outr = outi = None
    for i in range(6):
        vr, vi = xr[:, i][:, None], xi[:, i][:, None]
        if adjoint:
            cr, ci = mat[0, :, i], mat[1, :, i]
            tr, ti = cr * vr + ci * vi, cr * vi - ci * vr
        else:
            cr, ci = mat[0, :, :, i], mat[1, :, :, i]
            tr, ti = cr * vr - ci * vi, cr * vi + ci * vr
        outr, outi = (tr, ti) if outr is None else (outr + tr, outi + ti)
    return outr.reshape((4, 3) + tile), outi.reshape((4, 3) + tile)


def flip(v):
    return jnp.concatenate([v[:2], -v[2:]], axis=0)


def fan(ys, xs, cores, zs):
    offsets = [(y, x, c, z) for y in ys for x in xs for c in cores for z in zs if (y, x, c, z) != (0, 0, 0, 0)]
    return sorted(offsets, key=lambda o: -(min(o[0], 4 - o[0]) + min(o[1], 4 - o[1]) + min(o[3], 4 - o[3])))


ALONG_ROW = fan([0], range(4), range(2), [0])
ALONG_Y = fan(range(4), [0], [0], [0])
ALONG_Z = fan([0], [0], [0], range(4))
ALONG_SPACE = fan(range(4), range(4), range(2), [0])
EVERYONE = fan(range(4), range(4), range(2), range(4))
ROUNDS = (ALONG_ROW, ALONG_Y, ALONG_Z)


def kernel(
    n_space, n_tm,
    src_hbm, clov_hbm, link_hbm, mom_hbm, out_ref,
    src, clov, link, mom_ref, wlink, wclov, sfield, field, inner, base, bil, cur, phase_hi, phase_lo, momrow,
    send, recv, row_s, row_r0, row_r1, row_r2, last_r, alpha_ref, loop_s, loop_r, far_clov, far_link, far_send, far_recv, far_raw, echo, partial,
    in_sem, send_sem, recv_sem, row_ssem, row_rsem, loop_ssem, loop_rsem, far_ssem, far_rsem,
):
    x = lax.axis_index("space")
    t = lax.axis_index("tm")
    x_up, x_dn = lax.rem(x + 1, n_space), lax.rem(x + n_space - 1, n_space)
    t_up, t_dn = lax.rem(t + 1, n_tm), lax.rem(t + n_tm - 1, n_tm)

    loads = [
        pltpu.make_async_copy(a, b, in_sem.at[k])
        for k, (a, b) in enumerate(((src_hbm, src), (link_hbm, link), (clov_hbm, clov), (mom_hbm, mom_ref)))
    ]
    for load in loads:
        load.start()

    def space_at(dy, dx, dc):
        return ((x // 8 + dy) & 3) * 8 + (((x // 2) + dx) & 3) * 2 + ((x + dc) & 1)

    def place(offset):
        dy, dx, dc, dz = offset
        return (space_at(dy, dx, dc), (t + dz) & 3)

    barrier = pltpu.get_barrier_semaphore()
    greeted = [(x_up, t), (x_dn, t)] + [place(offset) for group in ROUNDS for offset in group]
    for device in greeted:
        pl.semaphore_signal(barrier, inc=1, device_id=device, device_id_type=MESH)

    lane = lax.broadcasted_iota(jnp.int32, (8, 128), 1)
    row = lax.broadcasted_iota(jnp.int32, (8, 128), 0)
    lane1 = lax.broadcasted_iota(jnp.int32, (1, 128), 1)
    zc = lane & 31
    yc = row * 4 + (lane >> 5)
    ev = ((yc + zc + x + t) & 1) == 0

    def move(v, axis, by):
        last = v.ndim - 1
        if axis == 2:
            if by == 1:
                return jnp.where(zc == 31, pltpu.roll(v, 31, last), pltpu.roll(v, 127, last))
            return jnp.where(zc == 0, pltpu.roll(v, 97, last), pltpu.roll(v, 1, last))
        if by == 1:
            a = pltpu.roll(v, 96, last)
            return jnp.where(lane >= 96, pltpu.roll(a, 7, last - 1), a)
        a = pltpu.roll(v, 32, last)
        return jnp.where(lane < 32, pltpu.roll(a, 1, last - 1), a)

    def cos_sin(k):
        a = (k - 16).astype(jnp.float32) * (math.pi / 32)
        q = a * a
        s = 1.0 / math.factorial(11)
        for m in (9, 7, 5, 3, 1):
            s = 1.0 / math.factorial(m) - q * s
        s = s * a
        c = 1.0 / math.factorial(12)
        for m in (10, 8, 6, 4, 2, 0):
            c = 1.0 / math.factorial(m) - q * c
        return 2.0 * s * s - 1.0, -2.0 * s * c

    def pack_clover(par):
        def step(k, carry):
            re_im, chi, r = k // 12, (k // 6) % 2, k % 6
            a = clov[re_im, chi, r]
            b = move(a, 2, -1)
            wclov[par, re_im, chi, r] = jnp.where(ev, a, b) if par == 0 else jnp.where(ev, b, a)
            return carry

        lax.fori_loop(0, 24, step, 0)

    t_sign = jnp.where(t == n_tm - 1, -1.0, 1.0).astype(jnp.float32)

    def pack_links(directions):
        for mu in directions:
            for re_im in range(2):
                a = link[mu, re_im]
                if mu == 3:
                    a = a * t_sign
                b = move(a, 2, -1)
                wlink[0, mu, re_im] = jnp.where(ev, a, b)
                wlink[1, mu, re_im] = jnp.where(ev, b, a)

    n_mom = mom_ref.shape[1]

    def make_phases():
        loads[3].wait()
        mom = mom_ref[...].astype(jnp.float32)
        eye = lax.broadcasted_iota(jnp.int32, (MOM, n_mom), 0) == lax.broadcasted_iota(jnp.int32, (MOM, n_mom), 1)
        columns = [
            jnp.sum(jnp.where(eye, jnp.broadcast_to(mom[k : k + 1], (MOM, n_mom)), 0.0), axis=1, keepdims=True).astype(jnp.int32)
            for k in range(3)
        ]
        zero_rows = jnp.zeros((64 - MOM, 2048), jnp.bfloat16)
        for ref in (phase_hi, phase_lo):
            ref[MOM:64, :] = zero_rows
            ref[64 + MOM : 128, :] = zero_rows

        def phases(s, carry):
            yrow = s * 4 + (lane1 >> 5)
            zrow = lane1 & 31
            c, sn = cos_sin((columns[0] * x + columns[1] * yrow + columns[2] * zrow) & 31)
            for value, places in ((c, ((0, 0, 1), (64, 128, 1))), (sn, ((0, 128, 1), (64, 0, -1)))):
                hi = value.astype(jnp.bfloat16)
                lo = (value - hi.astype(jnp.float32)).astype(jnp.bfloat16)
                for r0, c0, sign in places:
                    at = pl.ds(pl.multiple_of(s * 256 + c0, 128), 128)
                    phase_hi[r0 : r0 + MOM, at] = hi * sign
                    phase_lo[r0 : r0 + MOM, at] = lo * sign
            return carry

        lax.fori_loop(0, 8, phases, 0)
        momrow[...] = jnp.zeros_like(momrow)
        momrow[0:1, 0:n_mom] = mom[2:3]
        momrow[0:1, 64 : 64 + n_mom] = mom[2:3]
        loop_s[...] = jnp.zeros_like(loop_s)
        zero = jnp.zeros((4, 3, 8, 128), jnp.float32)
        field[5, 0] = zero
        field[5, 1] = zero

    def project(fr, fi, mu, sign):
        rows_r, rows_i = [], []
        for spin in range(2):
            col, power = UPPER[mu][spin]
            if sign < 0:
                power += 2
            r, i = add_times_i(power, (fr[spin], fi[spin]), (fr[2 + col], fi[2 + col]))
            rows_r.append(r)
            rows_i.append(i)
        return jnp.stack(rows_r), jnp.stack(rows_i)

    def add_up(acc, half, mu, sign):
        hr, hi = half
        for spin in range(2):
            acc[spin] = (hr[spin], hi[spin]) if acc[spin] is None else (acc[spin][0] + hr[spin], acc[spin][1] + hi[spin])
            col, power = LOWER[mu][spin]
            if sign < 0:
                power += 2
            term = (hr[col], hi[col])
            acc[2 + spin] = times_i(power, *term) if acc[2 + spin] is None else add_times_i(power, acc[2 + spin], term)

    def to_row(tiles):
        out = jnp.zeros((8, 128), jnp.float32)
        for k, tile in enumerate(tiles):
            for n in range(2):
                part = jnp.where(ev, tile, 0.0) if n == 0 else jnp.where(ev, 0.0, tile)
                out = jnp.where(row == 2 * k + n, jnp.sum(part, axis=0, keepdims=True), out)
        for by in (64, 32, 16):
            out = out + pltpu.roll(out, by, 1)
        return jnp.sum(jnp.where(lane >> 4 == row, out, 0.0), axis=0, keepdims=True)

    def from_row(line, k):
        return [
            jnp.sum(jnp.where(lane1 >> 4 == 2 * k + n, line, 0.0), axis=1, keepdims=True) for n in range(2)
        ]

    def row_send(group, slot, dst, stage):
        for k, offset in enumerate(group):
            pltpu.make_async_remote_copy(
                src_ref=row_s.at[slot, pl.ds(0, 1)], dst_ref=dst.at[pl.ds(k, 1)], send_sem=row_ssem.at[stage],
                recv_sem=row_rsem.at[stage], device_id=place(offset), device_id_type=MESH,
            ).start()

    def row_recv(slot, dst, stage):
        pltpu.make_async_copy(dst, dst, row_rsem.at[stage]).wait()
        return row_s[slot, 0:1, :] + jnp.sum(dst[...], axis=0, keepdims=True)

    first_r = (row_r0, row_r1, row_r2)

    def spread(pair):
        return jnp.where(ev, jnp.broadcast_to(pair[0], (8, 128)), jnp.broadcast_to(pair[1], (8, 128)))

    products = gamma_products()

    def project_loops(q, at_field, at_inner):
        for a in range(4):
            par_r, par_i = [], []
            for par, ref, at in ((0, field, at_field), (1, inner, at_inner)):
                br = bi = None
                for c in range(3):
                    sr, si = sfield[par, 0, a, c], sfield[par, 1, a, c]
                    pr, pi = ref[at, 0, :, c], ref[at, 1, :, c]
                    tr, ti = sr * pr + si * pi, sr * pi - si * pr
                    br, bi = (tr, ti) if br is None else (br + tr, bi + ti)
                par_r.append(br)
                par_i.append(bi)
            for re_im, (e, o) in enumerate((par_r, par_i)):
                bil[0, re_im, a] = jnp.where(ev, e, o)
                bil[1, re_im, a] = jnp.where(ev, o, e)

        def gammas(n, carry):
            for first in range(4):
                group = [g for g in range(16) if abs(products[g][0, first]) > 0.5]
                perm = [int(np.argmax(np.abs(products[group[0]][a]))) for a in range(4)]
                terms = [(bil[n, 0, a, perm[a]], bil[n, 1, a, perm[a]]) for a in range(4)]
                for g in group:
                    acc = None
                    for a in range(4):
                        power = int(round(np.angle(products[g][a, perm[a]]) / (math.pi / 2))) % 4
                        acc = times_i(power, *terms[a]) if acc is None else add_times_i(power, acc, terms[a])
                    for re_im in range(2):
                        start = pl.multiple_of((re_im * 32 + n * 16 + g) * 8, 8)
                        cur[pl.ds(start, 8), :] = acc[re_im]
            return carry

        lax.fori_loop(0, 2, gammas, 0)
        out = jnp.zeros((32, 128), jnp.float32)
        contract = (((1,), (1,)), ((), ()))
        for s in range(8):
            both = jnp.concatenate([cur[pl.ds(s, 32, stride=8), :], cur[pl.ds(256 + s, 32, stride=8), :]], axis=1)
            hi = both.astype(jnp.bfloat16)
            lo = (both - hi.astype(jnp.float32)).astype(jnp.bfloat16)
            wide = slice(s * 256, s * 256 + 256)
            ph, plo = phase_hi[:, wide], phase_lo[:, wide]
            main = lax.dot_general(jnp.concatenate([hi, lo], axis=0), ph, contract, preferred_element_type=jnp.float32)
            out = out + main[:32] + main[32:]
            out = out + lax.dot_general(hi, plo, contract, preferred_element_type=jnp.float32)
        loop_s[pl.ds(q, 32, stride=8), :] = out

    def loops_send():
        for k, offset in enumerate(ALONG_SPACE):
            target, _ = place(offset)
            pltpu.make_async_remote_copy(
                src_ref=loop_s.at[pl.ds(pl.multiple_of(target * 8, 8), 3)], dst_ref=loop_r.at[k, pl.ds(0, 3)],
                send_sem=loop_ssem, recv_sem=loop_rsem, device_id=(target, t), device_id_type=MESH,
            ).start()

    def main(core):
        far, near = (x_dn, x_up) if core == 0 else (x_up, x_dn)
        devices = ((far, t), (near, t), (x, t_dn), (x, t_up))
        sign_in = (1, -1, -1, 1) if core == 0 else (-1, 1, -1, 1)
        sign_out = (-1, 1, -1, 1) if core == 0 else (1, -1, -1, 1)
        axes = (0, 0, 3, 3)

        def copy(j, k, part):
            at = PARTS[k][part]
            return pltpu.make_async_remote_copy(
                src_ref=send.at[j, k, :, :, :, at], dst_ref=recv.at[j, k, :, :, :, at], send_sem=send_sem,
                recv_sem=recv_sem.at[j, k, part], device_id=devices[k], device_id_type=MESH,
            )

        def post(j, k, part, par, fr, fi):
            at = PARTS[k][part]
            half = project(fr, fi, axes[k], sign_out[k])
            if sign_out[k] > 0:
                half = color_apply(wlink.at[par, axes[k], :, :, :, at], half, True)
            send[j, k, 0, :, :, at] = half[0]
            send[j, k, 1, :, :, at] = half[1]
            copy(j, k, part).start()

        def take(acc, j, k, part, to):
            at = PARTS[k][part]
            copy(j, k, part).wait_recv()
            half = (recv[j, k, 0, :, :, at], recv[j, k, 1, :, :, at])
            if k == 0 and j > 0:
                half = (half[0] + echo[0, :, :, at], half[1] + echo[1, :, :, at])
            if sign_in[k] < 0:
                half = color_apply(wlink.at[to, axes[k], :, :, :, at], half, False)
            add_up(acc, half, axes[k], sign_in[k])

        def stacked(acc):
            return jnp.stack([a[0] for a in acc]), jnp.stack([a[1] for a in acc])

        def message(j, at=slice(0, 8)):
            if j == 0:
                return inner[4, 0, :, :, at], inner[4, 1, :, :, at]
            p = (j - 1) // 2
            if j % 2 == 0:
                return inner[p, 0, :, :, at], inner[p, 1, :, :, at]
            fr, fi = field[p, 0, :, :, at], field[p, 1, :, :, at]
            return (flip(fr), flip(fi)) if p % 2 == 0 else (fr, fi)

        def linear(j, fr, fi, clover):
            if j == 0:
                return KAPPA * fr, KAPPA * fi
            adjoint = (j - 1) // 2 % 2 == 0
            if j % 2 == 1:
                fr, fi = clover_apply(clover, fr, fi, adjoint)
                return KAPPA * fr, KAPPA * fi
            if adjoint:
                fr, fi = flip(fr), flip(fi)
            return -KAPPA * fr, -KAPPA * fi

        def outgoing(j, fr, fi):
            if j % 4 == 0:
                return flip(fr), flip(fi)
            return fr, fi

        def far_copy(k):
            src, dst = (far_send.at[k], far_recv.at[k]) if k < 2 else (link.at[0], far_raw)
            return pltpu.make_async_remote_copy(
                src_ref=src, dst_ref=dst, send_sem=far_ssem.at[k], recv_sem=far_rsem.at[k],
                device_id=devices[0], device_id_type=MESH,
            )

        def make_echo(j):
            par = j % 2
            if j == 1 and core == 0:
                far_copy(2).wait_recv()
                a = far_raw[...]
                b = move(a, 2, -1)
                far_link[0] = jnp.where(ev, b, a)
                far_link[1] = jnp.where(ev, a, b)
            if j == 2:
                for chi in range(2):
                    far_copy(chi).wait_recv()

                    def unpack(r, carry):
                        a = far_recv[chi, r]
                        far_clov[0, chi, r] = jnp.where(ev, a, move(a, 2, -1))
                        far_clov[1, chi, r] = jnp.where(ev, move(a, 2, 1), a)
                        return carry

                    lax.fori_loop(0, 6, unpack, 0)
            half = project(*message(j - 1), 0, sign_out[0])
            if core == 1:
                half = color_apply(wlink.at[par, 0], half, True)
            else:
                half = color_apply(far_link.at[1 - par], half, False)
            acc = [None] * 4
            add_up(acc, half, 0, sign_out[0])
            fr, fi = outgoing(j - 1, *linear(j - 1, *stacked(acc), far_clov))
            half = project(fr, fi, 0, sign_in[0])
            if core == 0:
                half = color_apply(far_link.at[1 - par], half, True)
            echo[0] = half[0]
            echo[1] = half[1]

        def early(j):
            if j == 0:
                if core == 1:
                    far_copy(2).start()
                pack_clover(1)
                for chi in range(2):

                    def pack(r, carry):
                        far_send[chi, r] = jnp.where(ev, wclov[1, 1, chi, r], wclov[1, 0, chi, r])
                        return carry

                    lax.fori_loop(0, 6, pack, 0)
                far_copy(0).start()
                pack_links((1, 2))
            if j == 1:
                far_copy(1).start()
            if j == 5:
                r0, r1 = field[1, 0], field[1, 1]
                i0, i1 = field[2, 0], field[2, 1]
                row_s[0, 0:1, :] = to_row([jnp.sum(a * a + b * b, axis=(0, 1)) for a, b in ((r0, r1), (i0, i1))])
                row_send(ROUNDS[0], 0, first_r[0], 0)
            if j in (6, 7):
                row_s[j - 5, 0:1, :] = row_recv(j - 6, first_r[j - 6], j - 6)
                row_send(ROUNDS[j - 5], j - 5, first_r[j - 5], j - 5)

        def late(j):
            if j == 0:
                pack_clover(0)
            if j == 1:
                make_phases()
            if j > 0 and j % 2 == 0:
                p = j // 2 - 1
                cr, ci = clover_apply(wclov.at[0], field[p, 0], field[p, 1], p % 2 == 0)
                base[0] = cr
                base[1] = ci
            if j == 4:
                project_loops(0, 5, 4)
            if j == 6:
                project_loops(1, 1, 1)
            if j == 8:
                line = row_recv(2, first_r[2], 2)
                row_s[3, 0:1, :] = line
                rr, image = from_row(line, 0), from_row(line, 1)
                alpha = spread([rr[n] / image[n] for n in range(2)])
                alpha_ref[0] = alpha
                alpha_odd = spread([rr[1 - n] / image[1 - n] for n in range(2)])
                sq = None
                for re_im in range(2):
                    r = field[1, re_im] - alpha * field[3, re_im]
                    field[6, re_im] = r
                    inner[5, re_im] = inner[1, re_im] - alpha_odd * inner[3, re_im]
                    part = jnp.sum(r * r, axis=(0, 1))
                    sq = part if sq is None else sq + part
                alpha_ref[1] = sq
                project_loops(2, 6, 5)
                loops_send()

        for part in range(2):
            post(0, 0, part, 1, *message(0, HALVES[part]))
        for part in range(2):
            for k in (2, 3):
                post(0, k, part, 1, *message(0, HALVES[part]))
        for j in range(9):
            par, to = 1 - j % 2, j % 2
            p = (j - 1) // 2
            fr, fi = message(j)
            post(j, 1, 0, par, fr, fi)
            early(j)
            acc = [None] * 4
            for mu in (1, 2):
                hr, hi = project(fr, fi, mu, -1)
                ahead = (move(hr, mu, 1), move(hi, mu, 1))
                add_up(acc, color_apply(wlink.at[to, mu], ahead, False), mu, -1)
                hr, hi = color_apply(wlink.at[par, mu], project(fr, fi, mu, 1), True)
                add_up(acc, (move(hr, mu, -1), move(hi, mu, -1)), mu, 1)
            if j > 0:
                make_echo(j)
            late(j)
            take(acc, j, 1, 0, to)
            partial[0], partial[1] = stacked(acc)
            for part, at in enumerate(HALVES):
                acc = [(partial[0, spin, :, at], partial[1, spin, :, at]) for spin in range(4)]
                for k in (2, 3):
                    take(acc, j, k, part, to)
                vr, vi = linear(j, *stacked(acc), wclov.at[1, :, :, :, :, at])
                if j % 2 == 0:
                    start, first = (base, ()) if j > 0 else (sfield, (0,))
                    vr = start[first + (0, slice(None), slice(None), at)] + vr
                    vi = start[first + (1, slice(None), slice(None), at)] + vi
                partial[0, :, :, at] = vr
                partial[1, :, :, at] = vi
                if j < 8:
                    post(j + 1, 0, part, to, *outgoing(j, vr, vi))
            for part, at in enumerate(HALVES):
                acc = [None] * 4
                take(acc, j, 0, part, to)
                lr, li = linear(j, *stacked(acc), wclov.at[1, :, :, :, :, at])
                vr, vi = partial[0, :, :, at] + lr, partial[1, :, :, at] + li
                if j == 8:
                    m1 = m2 = None
                    for re_im, v in ((0, vr), (1, vi)):
                        w = field[2, re_im, :, :, at]
                        v = w - alpha_ref[0, at] * v
                        a, b = jnp.sum(v * v, axis=(0, 1)), jnp.sum(v * w, axis=(0, 1))
                        m1, m2 = (a, b) if m1 is None else (m1 + a, m2 + b)
                    alpha_ref[2, at] = m1
                    alpha_ref[3, at] = m2
                else:
                    store, slot = (field, j // 2) if j % 2 == 0 else (inner, p)
                    store[slot, 0, :, :, at] = vr
                    store[slot, 1, :, :, at] = vi
                    for k in (2, 3):
                        post(j + 1, k, part, to, *outgoing(j, vr, vi))
        for k in range(2 + core):
            far_copy(k).wait_send()

    loads[0].wait()
    for re_im in range(2):
        a = src[0, re_im]
        b = move(src[1, re_im], 2, -1)
        sfield[0, re_im] = jnp.where(ev, a, b)
        sfield[1, re_im] = jnp.where(ev, b, a)
    loads[1].wait()
    pack_links((0, 3))
    loads[2].wait()
    both = [clover_apply(clov, src[n, 0], src[n, 1], False) for n in range(2)]
    for re_im in range(2):
        inner[4, re_im] = jnp.where(ev, move(both[1][re_im], 2, -1), both[0][re_im])
    pl.semaphore_wait(barrier, len(greeted))
    for core in range(2):
        pl.when(x % 2 == core)(lambda core=core: main(core))

    row_s[4, 0:1, :] = to_row([alpha_ref[1], alpha_ref[2], alpha_ref[3]])
    row_send(EVERYONE, 4, last_r, 3)
    second = x >= n_space // 2
    angle = momrow[0:1, :].astype(jnp.int32) * second.astype(jnp.int32)
    cos, sin = cos_sin(angle & 31)
    sin = jnp.where(lane1 < 64, -sin, sin)
    pieces = loop_r.at[:, pl.ds(0, 3)]
    pltpu.make_async_copy(pieces, pieces, loop_rsem).wait()
    own = loop_s[pl.ds(pl.multiple_of(x * 8, 8), 3), :]
    piece = own + jnp.sum(loop_r[:, 0:3, :], axis=0)
    piece = piece * cos + pltpu.roll(piece, 64, 1) * sin
    piece = piece * (1.0 / math.sqrt(n_space * NY * NZ))
    start = row_s[3, 0:1, :]
    rr0, im0 = [jnp.where(second, v[1], v[0]) for v in (from_row(start, 0), from_row(start, 1))]
    line = row_recv(4, last_r, 3)
    rr1, m1, m2 = [jnp.where(second, v[1], v[0]) for v in (from_row(line, 0), from_row(line, 1), from_row(line, 2))]
    alpha0, beta = rr0 / im0, rr1 / rr0
    alpha1 = rr1 / (m1 + beta * (2.0 * m2 + beta * im0))
    line = piece[0:1] + (alpha0 + alpha1 * beta) * piece[1:2] + alpha1 * piece[2:3]
    out_ref[0] = line[:, 0:n_mom]
    out_ref[1] = line[:, 64 : 64 + n_mom]

    pltpu.make_async_copy(send, send, send_sem).wait()
    for stage, ref in enumerate((row_r0, row_r1, row_r2, last_r)):
        pltpu.make_async_copy(ref, ref, row_ssem.at[stage]).wait()
    pltpu.make_async_copy(pieces, pieces, loop_ssem).wait()


def solution(mesh):
    n_space, n_tm = mesh.shape["space"], mesh.shape["tm"]

    def local(sources, links, clover, momenta):
        f32 = jnp.float32
        n_mom = momenta.shape[0]
        tile = (8, 128)
        scratch = [
            pltpu.VMEM((2, 2, 4, 3) + tile, f32),
            pltpu.VMEM((2, 2, 6, 6) + tile, f32),
            pltpu.VMEM((4, 2, 3, 3) + tile, f32),
            pltpu.VMEM((3, n_mom), jnp.int32),
            pltpu.VMEM((2, 4, 2, 3, 3) + tile, f32),
            pltpu.VMEM((2, 2, 2, 6, 6) + tile, f32),
            pltpu.VMEM((2, 2, 4, 3) + tile, f32),
            pltpu.VMEM((7, 2, 4, 3) + tile, f32),
            pltpu.VMEM((6, 2, 4, 3) + tile, f32),
            pltpu.VMEM((2, 4, 3) + tile, f32),
            pltpu.VMEM((2, 2, 4, 4) + tile, f32),
            pltpu.VMEM((512, 128), f32),
            pltpu.VMEM((128, 2048), jnp.bfloat16),
            pltpu.VMEM((128, 2048), jnp.bfloat16),
            pltpu.VMEM(tile, f32),
            pltpu.VMEM((9, 4, 2, 2, 3) + tile, f32),
            pltpu.VMEM((9, 4, 2, 2, 3) + tile, f32),
            pltpu.VMEM((6,) + tile, f32),
            *[pltpu.VMEM((len(group), 128), f32) for group in ROUNDS + (EVERYONE,)],
            pltpu.VMEM((4,) + tile, f32),
            pltpu.VMEM((256, 128), f32),
            pltpu.VMEM((n_space - 1,) + tile, f32),
            pltpu.VMEM((2, 2, 6, 6) + tile, f32),
            pltpu.VMEM((2, 2, 3, 3) + tile, f32),
            pltpu.VMEM((2, 6, 6) + tile, f32),
            pltpu.VMEM((2, 6, 6) + tile, f32),
            pltpu.VMEM((2, 3, 3) + tile, f32),
            pltpu.VMEM((2, 2, 3) + tile, f32),
            pltpu.VMEM((2, 4, 3) + tile, f32),
            pltpu.SemaphoreType.DMA((4,)),
            pltpu.SemaphoreType.DMA,
            pltpu.SemaphoreType.DMA((9, 4, 2)),
            pltpu.SemaphoreType.DMA((5,)),
            pltpu.SemaphoreType.DMA((5,)),
            pltpu.SemaphoreType.DMA,
            pltpu.SemaphoreType.DMA,
            pltpu.SemaphoreType.DMA((3,)),
            pltpu.SemaphoreType.DMA((3,)),
        ]
        out = pl.pallas_call(
            lambda *refs: kernel(n_space, n_tm, *refs),
            out_shape=jax.ShapeDtypeStruct((2, 1, n_mom), f32),
            in_specs=[pl.BlockSpec(memory_space=pl.ANY)] * 4,
            out_specs=pl.BlockSpec(memory_space=pltpu.VMEM),
            scratch_shapes=scratch,
            compiler_params=pltpu.CompilerParams(
                collective_id=0, has_side_effects=True, vmem_limit_bytes=48 * 1024 * 1024
            ),
            name="loops",
        )(
            *[
                pltpu.with_memory_space_constraint(v, pltpu.HBM)
                for v in (
                    sources.reshape((2, 2, 4, 3) + tile),
                    clover.reshape((2, 2, 6, 6) + tile),
                    links.reshape((4, 2, 3, 3) + tile),
                    momenta.T,
                )
            ]
        )
        return out.reshape(2, 1, n_mom, 1)

    placed = P(None, None, None, None, "space", "tm", None)
    return jax.shard_map(
        local, mesh=mesh, in_specs=(placed, placed, placed, P()), out_specs=P(None, "space", None, "tm"), check_vma=False
    )
```
